256 devices in a mesh: slab: 32 (over y, x, core), grp: 8 (over z).
Axes of the slice: x: 4, y: 4, z: 8, core: 2. Of those that a mesh axis runs over, the one named last changes fastest.
Arguments:
- right_side: float32 [64, 32768], P(None, ('slab', 'grp')), may hold values from -45 to 45
- stiffness: bfloat16 [7, 64, 64, 32768], P(None, None, None, ('slab', 'grp')), may hold values from -1 to 3.5
- columns: int32 [7, 32768], P(None, ('slab', 'grp')), may hold values from 0 to 1087, as said below
- margin_rows: int32 [32, 2, 32], P('slab'), may hold values from 0 to 1023, as said below
- local_inverse: bfloat16 [64, 64, 32768], P(None, None, ('slab', 'grp')), may hold values from -1 to 1.5
- margin_inverse: bfloat16 [64, 64, 2048], P(None, None, 'slab'), may hold values from -1 to 1.5
- basis: bfloat16 [64, 64, 32768], P(None, None, ('slab', 'grp')), may hold values from -0.0234375 to 0.0234375
- coarse_counts: int32 [32], P('slab'), may hold values from 32 to 64
- coarse_inverse: float32 [2048, 2048], P('slab'), may hold values from -65 to 65
Outputs:
- solution_field: float32 [64, 32768], P(None, ('slab', 'grp'))
- residual: float32 [64, 32768], P(None, ('slab', 'grp'))
- direction: float32 [64, 32768], P(None, ('slab', 'grp'))
The draws below stay inside these ranges and needn't reach their ends.
Inputs may be any that keep to these rules, and one draw needn't show every extreme that they name: Entry 0 of block row b names the row itself; every position of the last 32 columns of ext_s is named by some row of slab s, and so is every position of the first 32. margin_rows[s, 0] holds 32 distinct rows of the lowest quarter of slab s, margin_rows[s, 1] 32 distinct rows of its highest quarter.
All inputs are finite; a program needn't handle non-finite values.
Results may differ from the reference program's by a relative error of at most 0.0003.
Values sent between devices are 32-bit elements; how exact they have to be, the bound alone decides.
No kernel may reach another device: no remote copies, remote signals or barrier semaphores. Data moves between devices by JAX's collectives and lax.ppermute only.
A program may use at most 64 MiB of HBM per device.

```python
import math
import jax
import jax.numpy as jnp
from jax import lax

BS = 64
NNZ = 7
NCMAX = 64
ITERS = 2
NBS = 1024
NB = 32768
OV = 32
NC = 2048
N_SLAB = 32


def spread_scales(key, how_many, lowest, highest):
    return jnp.exp(jax.random.uniform(key, (how_many,), jnp.float32, math.log(lowest), math.log(highest)))


def inverse_blocks(key, how_many, exponent):
    key_scale, key_noise = jax.random.split(key)
    diagonal = spread_scales(key_scale, how_many, 0.25, 1.0)
    noise_part = jax.random.uniform(key_noise, (BS, BS, how_many), jnp.float32, -1.0, 1.0)
    noise_part = jnp.sign(noise_part) * jnp.abs(noise_part) ** exponent
    identity = jnp.eye(BS, dtype=jnp.float32)[:, :, None]
    return ((identity + 0.9 / BS * noise_part) * diagonal[None, None, :]).astype(jnp.bfloat16)


def draw_right_side(key, part):
    key = jax.random.fold_in(key, 5)
    key_values, key_scale = jax.random.split(key)
    slabs_total = NB // NBS
    slab_of = (jnp.arange(NB) // NBS).astype(jnp.float32)
    rising = 1.0 + 2.0 * slab_of / max(slabs_total - 1, 1)
    values = jax.random.truncated_normal(key_values, -4.0, 4.0, (BS, NB), jnp.float32)
    scales = spread_scales(key_scale, NB, 1.0, 3.3) * rising
    return values * scales[None, :]


def draw_stiffness(key, part):
    key = jax.random.fold_in(key, 11)
    key_diag, key_noise, key_couple = jax.random.split(key, 3)
    diagonal = spread_scales(key_diag, NB, 2.5, 3.4)
    coupling = spread_scales(key_couple, NNZ * NB, 0.05, 0.2).reshape(NNZ, NB)
    exponent = 1.0
    noise_part = jax.random.uniform(key_noise, (NNZ, BS, BS, NB), jnp.float32, -1.0, 1.0)
    noise_part = jnp.sign(noise_part) * jnp.abs(noise_part) ** exponent
    first = (jnp.arange(NNZ) == 0).astype(jnp.float32)
    centre = first[:, None] * diagonal[None, :] - (1.0 - first)[:, None] * coupling
    scales = (first * (0.2 / BS) + (1.0 - first) * (0.5 / BS))[:, None, None, None]
    identity = jnp.eye(BS, dtype=jnp.float32)[None, :, :, None] * centre[:, None, None, :]
    return (identity + scales * noise_part).astype(jnp.bfloat16)


def draw_columns(key, part):
    key = jax.random.fold_in(key, 41)
    key_perm, key_low, key_high = jax.random.split(key, 3)
    slabs_total = NB // NBS
    perm_keys = jax.random.split(key_perm, slabs_total * NNZ)
    shuffled = jax.vmap(lambda one_key: jax.random.permutation(one_key, NBS))(perm_keys)
    shuffled = shuffled.reshape(slabs_total, NNZ, NBS).astype(jnp.int32)
    lower_perm = jax.vmap(lambda one_key: jax.random.permutation(one_key, OV))(jax.random.split(key_low, slabs_total)).astype(jnp.int32)
    upper_perm = jax.vmap(lambda one_key: jax.random.permutation(one_key, OV))(jax.random.split(key_high, slabs_total)).astype(jnp.int32)
    positions = jnp.arange(NBS, dtype=jnp.int32)
    result = OV + shuffled
    result = result.at[:, 0, :].set(jnp.broadcast_to(OV + positions, (slabs_total, NBS)))
    filler = jnp.zeros((slabs_total, NBS - OV), jnp.int32)
    lower_full = jnp.concatenate([lower_perm, filler], axis=1)
    upper_full = jnp.concatenate([filler, OV + NBS + upper_perm], axis=1)
    last_column = result[:, NNZ - 1, :]
    last_column = jnp.where(positions[None, :] < OV, lower_full, last_column)
    last_column = jnp.where(positions[None, :] >= NBS - OV, upper_full, last_column)
    result = result.at[:, NNZ - 1, :].set(last_column)
    return jnp.transpose(result, (1, 0, 2)).reshape(NNZ, NB).astype(jnp.int32)


def draw_margin_rows(key, part):
    key = jax.random.fold_in(key, 51)
    slabs_total = NB // NBS
    quarter = NBS // 4

    def face_rows(one_key, forced):
        key_pick, key_order = jax.random.split(one_key)
        chosen = jax.random.permutation(key_pick, quarter)[:OV].astype(jnp.int32)
        has_zero = jnp.any(chosen == 0)
        with_zero = chosen.at[0].set(0)
        chosen = jnp.where(jnp.logical_and(forced, jnp.logical_not(has_zero)), with_zero, chosen)
        return chosen[jax.random.permutation(key_order, OV)]
    forced_flags = jnp.arange(2 * slabs_total) < 2
    rows_drawn = jax.vmap(face_rows)(jax.random.split(key, 2 * slabs_total), forced_flags).reshape(slabs_total, 2, OV)
    rows_drawn = rows_drawn.at[:, 1, :].set(NBS - 1 - rows_drawn[:, 1, :])
    return rows_drawn.astype(jnp.int32)


def draw_local_inverse(key, part):
    key = jax.random.fold_in(key, 21)
    return inverse_blocks(key, NB, 1.0)


def draw_margin_inverse(key, part):
    key = jax.random.fold_in(key, 22)
    slabs_total = NB // NBS
    return inverse_blocks(key, 2 * OV * slabs_total, 1.0)


def draw_coarse_counts(key, part):
    key = jax.random.fold_in(key, 61)
    key_values, key_pick = jax.random.split(key)
    slabs_total = NC // NCMAX
    kept = jax.random.randint(key_values, (slabs_total,), NCMAX // 2, NCMAX + 1).astype(jnp.int32)
    picked = jax.random.permutation(key_pick, slabs_total)
    kept = kept.at[picked[0]].set(NCMAX).at[picked[1]].set(NCMAX // 2)
    return kept.astype(jnp.int32)


def draw_coarse_inverse(key, part):
    key = jax.random.fold_in(key, 31)
    key_scale, key_sign = jax.random.split(key)
    slabs_total = NC // NCMAX
    scale_vector = spread_scales(key_scale, NC, 1.0, 4.0)
    decay = 2.0 / slabs_total
    signs = jnp.where(jax.random.uniform(key_sign, (NC,), jnp.float32) < 0.5, -1.0, 1.0)
    factor = scale_vector * signs
    index_all = jnp.arange(NC)
    slab_pos = (index_all // NCMAX).astype(jnp.float32)
    slot_pos = (index_all % NCMAX).astype(jnp.float32)
    kernel = jnp.exp(-jnp.abs(slab_pos[:, None] - slab_pos[None, :]) * decay - jnp.abs(slot_pos[:, None] - slot_pos[None, :]) / 4.0)
    return kernel * factor[:, None] * factor[None, :] + 0.5 * jnp.eye(NC, dtype=jnp.float32)


def steps_of(stream_key, extent, pieces, low, largest):
    loudness, own = 1.0, jax.random.fold_in(stream_key, 6)
    for axis_at, blocks in pieces:
        draws = jnp.exp(jax.random.uniform(jax.random.fold_in(own, axis_at), (blocks,), jnp.float32, low / len(pieces), largest / len(pieces)))
        loudness = loudness * jnp.repeat(draws, extent[axis_at] // blocks).reshape([-1 if axis == axis_at else 1 for axis in range(len(extent))])
    return loudness


def noise(rng, extent, deviation, reach, cuts=(), held_as=jnp.bfloat16):
    gain = steps_of(rng, extent, cuts, -0.22, 0.18) if cuts else 1.0
    entries = jax.random.normal(rng, extent, jnp.float32) * deviation * gain
    return jnp.minimum(jnp.maximum(entries, -reach), reach).astype(held_as)


def setup_inputs(seed: int = 0) -> dict:
    seeds = jax.random.split(jax.random.key(seed), 10)
    right_side = draw_right_side(jax.random.fold_in(seeds[9], 71), 0)
    stiffness = draw_stiffness(jax.random.fold_in(seeds[9], 71), 0)
    columns = draw_columns(jax.random.fold_in(seeds[9], 71), 0)
    margin_rows = draw_margin_rows(jax.random.fold_in(seeds[9], 71), 0)
    local_inverse = draw_local_inverse(jax.random.fold_in(seeds[9], 71), 0)
    margin_inverse = draw_margin_inverse(jax.random.fold_in(seeds[9], 71), 0)
    basis = noise(seeds[6], (NCMAX, BS, NB), (BS * NBS) ** -0.5, 0.0234375, ((2, 256),))
    coarse_counts = draw_coarse_counts(jax.random.fold_in(seeds[9], 71), 0)
    coarse_inverse = draw_coarse_inverse(jax.random.fold_in(seeds[9], 71), 0)
    return dict(right_side=right_side, stiffness=stiffness, columns=columns, margin_rows=margin_rows, local_inverse=local_inverse, margin_inverse=margin_inverse, basis=basis, coarse_counts=coarse_counts, coarse_inverse=coarse_inverse)


precise = lax.Precision.HIGHEST


def neighbour_rows(slab_values, margin_rows):
    face_width = margin_rows.shape[2]
    sent_down = jnp.take_along_axis(slab_values, margin_rows[None, :, 0, :], axis=2)
    sent_up = jnp.take_along_axis(slab_values, margin_rows[None, :, 1, :], axis=2)
    empty = jnp.zeros((slab_values.shape[0], 1, face_width), jnp.float32)
    lower_rim = jnp.concatenate([empty, sent_up[:, :-1]], axis=1)
    upper_rim = jnp.concatenate([sent_down[:, 1:], empty], axis=1)
    return lower_rim, upper_rim


def apply_stiffness(vector, stiffness, columns, margin_rows):
    slab_values = vector.reshape(BS, N_SLAB, NBS)
    lower_rim, upper_rim = neighbour_rows(slab_values, margin_rows)
    extended = jnp.concatenate([lower_rim, slab_values, upper_rim], axis=2)

    def one_slab(index):
        start = (index * NBS).astype(jnp.int32)
        blocks = lax.dynamic_slice_in_dim(stiffness, start, NBS, 3).astype(jnp.float32)
        named = lax.dynamic_slice_in_dim(columns, start, NBS, 1)
        values = lax.dynamic_index_in_dim(extended, index, 1, keepdims=False)
        picked = jnp.take(values, named, axis=1)
        return jnp.einsum('kijb,jkb->ib', blocks, picked, precision=precise)

    result = lax.map(one_slab, jnp.arange(N_SLAB, dtype=jnp.int32))
    return jnp.moveaxis(result, 0, 1).reshape(BS, NB)


def apply_preconditioner(vector, margin_rows, local_inverse, margin_inverse, basis, coarse_counts, coarse_inverse):
    slab_values = vector.reshape(BS, N_SLAB, NBS)
    lower_rim, upper_rim = neighbour_rows(slab_values, margin_rows)
    indices = jnp.arange(N_SLAB, dtype=jnp.int32)

    def one_slab(index):
        start = (index * NBS).astype(jnp.int32)
        inverse = lax.dynamic_slice_in_dim(local_inverse, start, NBS, 2).astype(jnp.float32)
        vectors = lax.dynamic_slice_in_dim(basis, start, NBS, 2).astype(jnp.float32)
        values = lax.dynamic_index_in_dim(slab_values, index, 1, keepdims=False)
        local_part = jnp.einsum('ijb,jb->ib', inverse, values, precision=precise)
        projected = jnp.einsum('jib,ib->j', vectors, values, precision=precise)
        return local_part, projected

    local_part, projected = lax.map(one_slab, indices)
    facing = jnp.concatenate([lower_rim, upper_rim], axis=2)
    blocks = margin_inverse.astype(jnp.float32).reshape(BS, BS, N_SLAB, 2 * OV)
    solved = jnp.einsum('ijsb,jsb->isb', blocks, facing, precision=precise)
    empty = jnp.zeros((BS, 1, OV), jnp.float32)
    from_below = jnp.concatenate([empty, solved[:, :-1, OV:]], axis=1)
    from_above = jnp.concatenate([solved[:, 1:, :OV], empty], axis=1)
    slab_index = indices[:, None]
    returned = jnp.zeros((BS, N_SLAB, NBS), jnp.float32)
    returned = returned.at[:, slab_index, margin_rows[:, 0, :]].add(from_below)
    returned = returned.at[:, slab_index, margin_rows[:, 1, :]].add(from_above)
    live_slots = (jnp.arange(NCMAX, dtype=jnp.int32)[None, :] < coarse_counts[:, None]).astype(jnp.float32)
    weights = jnp.dot(coarse_inverse, (projected * live_slots).reshape(NC), precision=precise)
    weights = weights.reshape(N_SLAB, NCMAX) * live_slots

    def expand(index):
        start = (index * NBS).astype(jnp.int32)
        vectors = lax.dynamic_slice_in_dim(basis, start, NBS, 2).astype(jnp.float32)
        return jnp.einsum('jib,j->ib', vectors, weights[index], precision=precise)

    coarse_part = lax.map(expand, indices)
    total = jnp.moveaxis(local_part, 0, 1) + returned + jnp.moveaxis(coarse_part, 0, 1)
    return total.reshape(BS, NB)


def reference(right_side, stiffness, columns, margin_rows, local_inverse, margin_inverse, basis, coarse_counts, coarse_inverse):
    def precondition(vector):
        return apply_preconditioner(vector, margin_rows, local_inverse, margin_inverse, basis, coarse_counts, coarse_inverse)

    solution_field = jnp.zeros_like(right_side)
    residual = right_side
    search = precondition(residual)
    direction = search
    energy = jnp.sum(residual * search)
    for iteration in range(ITERS):
        image = apply_stiffness(direction, stiffness, columns, margin_rows)
        step_size = energy / jnp.sum(direction * image)
        solution_field = solution_field + step_size * direction
        residual = residual - step_size * image
        search = precondition(residual)
        energy_next = jnp.sum(residual * search)
        direction = search + (energy_next / energy) * direction
        energy = energy_next
    return solution_field, residual, direction
```

```python
import jax
import jax.numpy as jnp
from jax import lax
from jax.sharding import PartitionSpec as P

AXES = ("slab", "grp")
precise = lax.Precision.HIGHEST


def ein(pattern, *operands):
    return jnp.einsum(pattern, *operands, precision=precise, preferred_element_type=jnp.float32)


def local(
    right_side,
    stiffness,
    columns,
    margin_rows,
    local_inverse,
    margin_inverse,
    basis,
    coarse_counts,
    coarse_inverse,
):
    slabs, groups = lax.axis_size("slab"), lax.axis_size("grp")
    width = margin_rows.shape[2]
    size, rows = right_side.shape
    modes = basis.shape[0]
    group = lax.axis_index("grp")
    half = groups // 2
    is_low = group < half
    face_rows = jnp.where(is_low, margin_rows[0, 0], margin_rows[0, 1]) - group * rows
    select = (face_rows[:, None] == jnp.arange(rows, dtype=jnp.int32)[None, :]).astype(jnp.float32)
    live = (jnp.arange(modes, dtype=jnp.int32) < coarse_counts[0]).astype(jnp.float32)

    def pairs(low_step):
        found = []
        for s in range(slabs):
            for g in range(groups):
                other = s + (low_step if g < half else -low_step)
                if 0 <= other < slabs:
                    found.append((s * groups + g, other * groups + g))
        return found

    blocks = jnp.where(is_low, margin_inverse[:, :, width:], margin_inverse[:, :, :width])
    blocks = lax.ppermute(blocks.astype(jnp.float32), AXES, pairs(1))
    inverse = local_inverse.astype(jnp.float32) + ein("ijt,tb->ijb", blocks, select)

    def project(vector):
        return ein("jib,ib->j", basis, vector) * live

    def share(projected, dots):
        row = jnp.concatenate([projected, jnp.stack(dots)]) if dots else projected
        row = jnp.pad(row, (0, 128 - row.shape[0]))
        table = jnp.broadcast_to(row[None, :], (slabs * groups, 128))
        table = lax.all_to_all(table, AXES, 0, 0).reshape(slabs, groups, 128).sum(axis=1)
        totals = table[:, modes:].sum(axis=0)
        mine = lax.dynamic_index_in_dim(table, lax.axis_index("slab"), 0, keepdims=False)[:modes]
        weights = ein("jn,n->j", coarse_inverse, table[:, :modes].reshape(-1)) * live
        return mine, weights, totals

    def expand(weights):
        return ein("jib,j->ib", basis, weights)

    def solve_local(vector):
        return ein("ijb,jb->ib", inverse, vector)

    def stiff(vector):
        rim = lax.ppermute(ein("ib,tb->it", vector, select), AXES, pairs(-1))
        sent = jnp.concatenate([vector, rim], axis=1)
        sent = jnp.broadcast_to(sent[None], (groups,) + sent.shape)
        got = lax.all_to_all(sent, "grp", 0, 0)
        own = jnp.moveaxis(got[:, :, :rows], 0, 1).reshape(size, groups * rows)
        upper = got[:half, :, rows:].sum(axis=0)
        lower = got[half:, :, rows:].sum(axis=0)
        extended = jnp.concatenate([lower, own, upper], axis=1)
        return ein("kijb,jkb->ib", stiffness, jnp.take(extended, columns, axis=1))

    def dot(a, b):
        return jnp.sum(a * b)

    r0 = right_side
    p_r0, w_r0, _ = share(project(r0), [])
    z0 = solve_local(r0) + expand(w_r0)

    q0 = stiff(z0)
    p_q0, w_q0, t = share(project(q0), [dot(r0, z0), dot(z0, q0)])
    e0, z0q0 = t[0], t[1]
    m0 = solve_local(q0) + expand(w_q0)
    step0 = e0 / z0q0
    r1 = r0 - step0 * q0
    z1 = z0 - step0 * m0

    y1 = stiff(z1)
    s_y1 = solve_local(y1)
    dots = [dot(r1, z1), dot(z1, y1), dot(z1, q0), dot(z0, y1), dot(r1, s_y1), dot(y1, s_y1)]
    dots += [dot(q0, s_y1), dot(r1, m0), dot(y1, m0), dot(q0, m0)]
    p_y1, w_y1, t = share(project(y1), dots)
    e1, z1y1, z1q0, z0y1, r1s, y1s, q0s, r1m0, y1m0, q0m0 = (t[i] for i in range(len(dots)))
    beta0 = e1 / e0
    step1 = e1 / (z1y1 + beta0 * (z1q0 + z0y1) + beta0 * beta0 * z0q0)
    d1 = z1 + beta0 * z0
    q1 = y1 + beta0 * q0
    x2 = step0 * z0 + step1 * d1
    r2 = r1 - step1 * q1
    z2 = z1 - step1 * (s_y1 + expand(w_y1) + beta0 * m0)

    p_r1 = p_r0 - step0 * p_q0
    p_q1 = p_y1 + beta0 * p_q0
    coarse = jnp.sum((step1 * p_q1 - p_r1) * w_y1)
    coarse = jnp.broadcast_to(coarse, (slabs, 1, 128))
    coarse = lax.all_to_all(coarse, "slab", 0, 0).sum(axis=0)[0, 0]
    q1m1 = y1s + beta0 * (y1m0 + q0s) + beta0 * beta0 * q0m0
    e2 = e1 + step1 * (coarse + step1 * q1m1 - (z1y1 + beta0 * z1q0) - (r1s + beta0 * r1m0))
    return x2, r2, z2 + e2 / e1 * d1


def solution(mesh):
    in_specs = (
        P(None, AXES),
        P(None, None, None, AXES),
        P(None, AXES),
        P("slab", None, None),
        P(None, None, AXES),
        P(None, None, "slab"),
        P(None, None, AXES),
        P("slab"),
        P("slab", None),
    )
    out_specs = (P(None, AXES),) * 3
    return jax.shard_map(local, mesh=mesh, in_specs=in_specs, out_specs=out_specs, check_vma=False)
```

```python
import functools

import jax
import jax.numpy as jnp
from jax import lax
from jax.experimental import pallas as pl
from jax.experimental.pallas import tpu as pltpu
from jax.sharding import PartitionSpec as P

AXES = ("slab", "grp")
F32, I32 = jnp.float32, jnp.int32
LANES = 128
VMEM = pl.BlockSpec(memory_space=pltpu.VMEM)
SMEM = pl.BlockSpec(memory_space=pltpu.SMEM)
precise = lax.Precision.HIGHEST


def call(body, outs, specs, *operands, scratch=(), flops=0, **static):
    shapes = [jax.ShapeDtypeStruct(shape, dtype) for shape, dtype in outs]
    read = sum(x.size * x.dtype.itemsize for x in operands)
    return pl.pallas_call(
        functools.partial(body, **static),
        out_shape=shapes,
        in_specs=specs,
        out_specs=[VMEM] * len(shapes),
        scratch_shapes=list(scratch),
        cost_estimate=pl.CostEstimate(flops=flops, bytes_accessed=read, transcendentals=0),
    )(*operands)


def tile_sum(parts):
    return jnp.concatenate([jnp.sum(part, axis=0, keepdims=True) for part in parts], axis=0)


def lane_index(rows=8):
    return lax.broadcasted_iota(I32, (rows, LANES), 1)


def pick_lanes(block, index):
    index = jnp.broadcast_to(index, block.shape)
    return jnp.take_along_axis(block, index, axis=1, mode="promise_in_bounds")


def total(a, b):
    return jnp.sum(a * b, axis=0, keepdims=True)


def project_into(sums_ref, basis_ref, vector):
    modes, size, _ = basis_ref.shape

    def eight(step, carry):
        first = pl.multiple_of(step * 8, 8)
        parts = []
        for r in range(8):
            acc = jnp.zeros((16, LANES), F32)
            for t in range(0, size, 16):
                acc += basis_ref[first + r, t : t + 16, :].astype(F32) * vector[t : t + 16]
            parts.append(acc)
        sums_ref[pl.ds(first, 8), :] = tile_sum(parts)
        return carry

    lax.fori_loop(0, modes // 8, eight, 0)


def block_product(out_ref, blocks_ref, vector):
    size = blocks_ref.shape[0]

    def eight(step, carry):
        first = pl.multiple_of(step * 8, 8)
        parts = []
        for r in range(8):
            acc = jnp.zeros((8, LANES), F32)
            for t in range(0, size, 8):
                acc += blocks_ref[first + r, t : t + 8, :] * vector[t : t + 8]
            parts.append(acc)
        out_ref[pl.ds(first, 8), :] = tile_sum(parts)
        return carry

    lax.fori_loop(0, size // 8, eight, 0)


def write_table(table_ref, sums_ref, count, modes, dots):
    rest = LANES - modes
    rows = dots + [jnp.zeros((1, LANES), F32)] * (rest - len(dots))
    sums_ref[modes:, :] = jnp.concatenate(rows, axis=0)
    row = lax.dot_general(
        jnp.ones((8, LANES), F32),
        sums_ref[...],
        (((1,), (1,)), ((), ())),
        precision=precise,
        preferred_element_type=F32,
    )
    lane = lane_index()
    row = jnp.where((lane < count) | (lane >= modes), row, 0.0)
    for m in range(table_ref.shape[0] // 8):
        table_ref[8 * m : 8 * m + 8, :] = row


def begin_body(
    place, margin_rows, counts, field, basis, margin, table, packed, meta, sums, *, groups, rows
):
    size = field.shape[0]
    width = margin_rows.shape[2]
    group = place[0]
    face = jnp.where(group < groups // 2, 0, 1)
    project_into(sums, basis, field[...])
    write_table(table, sums, counts[0], basis.shape[0], [])

    lane = lane_index(1)
    slot, owned = jnp.zeros((1, LANES), I32), jnp.zeros((1, LANES), I32)
    source = jnp.full((1, LANES), -1, I32)
    for t in range(width):
        row = margin_rows[0, face, t] - group * rows
        hit = lane == row
        slot = jnp.where(hit, t, slot)
        owned = jnp.where(hit, 1, owned)
        source = jnp.where(lane % width == t, row, source)
    inside = ((source >= 0) & (source < rows)).astype(I32)
    source = jnp.clip(source, 0, rows - 1)
    meta[...] = jnp.concatenate([slot, owned, source, inside, jnp.zeros((4, LANES), I32)], axis=0)

    parts = LANES // width
    depth = size // parts
    lanes = lane_index(depth)
    full = LANES // margin.shape[2]

    def one(i, carry):
        result = jnp.zeros((depth, LANES), F32)
        for a in range(parts):
            block = margin[i, a * depth : (a + 1) * depth, :].astype(F32)
            block = jnp.concatenate([block] * full, axis=1)
            upper = pltpu.roll(block, (a * width - width) % LANES, 1)
            lower = pltpu.roll(block, a * width, 1)
            part = jnp.where(face == 0, upper, lower)
            result = jnp.where((lanes >= a * width) & (lanes < (a + 1) * width), part, result)
        packed[i] = result
        return carry

    lax.fori_loop(0, size, one, 0, unroll=4)


def inverse_body(meta, local_inverse, packed, field, inverse, solved, *, width):
    size, depth, _ = packed.shape
    slot = meta[0:1, :]
    owned = jnp.broadcast_to(meta[1:2, :], (depth, LANES)) > 0

    def one(i, carry):
        block = packed[i]
        for a in range(size // depth):
            extra = jnp.where(owned, pick_lanes(block, slot + a * width), 0.0)
            own = local_inverse[i, a * depth : (a + 1) * depth, :].astype(F32)
            inverse[i, a * depth : (a + 1) * depth, :] = own + extra
        return carry

    lax.fori_loop(0, size, one, 0, unroll=4)
    block_product(solved, inverse, field[...])


def coarse_weights(weights_ref, table, coarse, count):
    modes = coarse.shape[0]
    lane = lane_index()
    accs = [jnp.zeros((8, LANES), F32) for _ in range(modes // 8)]
    totals = jnp.zeros((8, LANES), F32)
    for m in range(table.shape[0] // 16):
        even, odd = table[16 * m : 16 * m + 8, :], table[16 * m + 8 : 16 * m + 16, :]
        totals += even + odd
        both = jnp.where(lane < modes, even, pltpu.roll(odd, modes, 1))
        both = jnp.sum(both, axis=0, keepdims=True)
        for r in range(modes // 8):
            accs[r] += coarse[8 * r : 8 * r + 8, LANES * m : LANES * m + LANES] * both
    weights = jnp.dot(
        jnp.concatenate(accs, axis=0),
        jnp.ones((LANES, LANES), F32),
        precision=precise,
        preferred_element_type=F32,
    )
    rows = lax.broadcasted_iota(I32, (modes, LANES), 0)
    weights_ref[...] = jnp.where(rows < count, weights, 0.0)
    return jnp.sum(totals, axis=0, keepdims=True)


def expand(weights_ref, basis):
    modes, size, _ = basis.shape

    def eight(step, accs):
        first = pl.multiple_of(step * 8, 8)
        weights = weights_ref[pl.ds(first, 8), :]
        accs = list(accs)
        for r in range(8):
            weight = weights[r : r + 1, :]
            for t in range(size // 16):
                accs[t] += basis[first + r, 16 * t : 16 * t + 16, :].astype(F32) * weight
        return tuple(accs)

    accs = tuple(jnp.zeros((16, LANES), F32) for _ in range(size // 16))
    return jnp.concatenate(lax.fori_loop(0, modes // 8, eight, accs), axis=0)


def own_row(table, slab):
    return jnp.sum(table[pl.ds(pl.multiple_of(slab * 8, 8), 8), :], axis=0, keepdims=True)


def spread(row, lane):
    return jnp.broadcast_to(row[:, lane : lane + 1], (1, LANES))


def send_out(vector, meta, rim, send, *, width):
    size = vector.shape[0]
    depth = rim.shape[0]
    picked = pick_lanes(vector, meta[2:3, :])
    picked = jnp.where(jnp.broadcast_to(meta[3:4, :], picked.shape) > 0, picked, 0.0)
    lanes = lane_index(depth)
    result = jnp.zeros((depth, LANES), F32)
    for a in range(size // depth):
        part = picked[a * depth : (a + 1) * depth]
        result = jnp.where((lanes >= a * width) & (lanes < (a + 1) * width), part, result)
    rim[...] = result
    for g in range(send.shape[0]):
        send[g, :size, :] = vector
        send[g, size:, :] = result


def first_body(
    place, counts, table, coarse, basis, solved, meta, search, mine, rim, send, weights, *, width
):
    coarse_weights(weights, table, coarse, counts[0])
    mine[...] = jnp.broadcast_to(own_row(table, place[1]), (8, LANES))
    search[...] = solved[...] + expand(weights, basis)
    send_out(search[...], meta, rim, send, width=width)


def second_body(
    place,
    counts,
    table,
    coarse,
    basis,
    solved,
    meta,
    field,
    search,
    image,
    mine0,
    answer,
    residual,
    search1,
    mine,
    scalars,
    rim,
    send,
    weights,
    *,
    width,
):
    modes = basis.shape[0]
    totals = coarse_weights(weights, table, coarse, counts[0])
    energy, curve = spread(totals, modes), spread(totals, modes + 1)
    step = energy / curve
    p_q0 = own_row(table, place[1])
    p_r1 = mine0[0:1, :] - step * p_q0
    mine[...] = jnp.concatenate([p_r1, p_q0, jnp.zeros((6, LANES), F32)], axis=0)
    scalars[...] = jnp.concatenate([energy, curve, step, jnp.zeros((5, LANES), F32)], axis=0)
    answer[...] = solved[...] + expand(weights, basis)
    residual[...] = field[...] - step * image[...]
    search1[...] = search[...] - step * answer[...]
    send_out(search1[...], meta, rim, send, width=width)


def pick_columns(got, columns, own, picked, width):
    groups, _, _ = got.shape
    size = own.shape[0]
    rows = LANES
    depth = got.shape[1] - size
    half = groups // 2
    upper = sum(got[g, size:, :] for g in range(half))
    lower = sum(got[g, size:, :] for g in range(half, groups))
    lanes = lane_index(depth)
    rims = []
    for a in range(size // depth):
        low = pltpu.roll(lower, (-a * width) % LANES, 1)
        high = pltpu.roll(upper, (width - a * width) % LANES, 1)
        rims.append(jnp.where(lanes < width, low, high))
    rims = jnp.concatenate(rims, axis=0)
    picked[0] = own[...]
    for k in range(1, columns.shape[0]):
        named = columns[k : k + 1, :] - width
        block = named // rows
        lane = named - block * rows
        inside = (named >= 0) & (named < groups * rows)
        rim_lane = jnp.where(named < 0, named + width, named - groups * rows + width)
        lane = jnp.where(inside, lane, rim_lane)
        block = jnp.broadcast_to(jnp.where(inside, block, groups), (8, LANES))
        lane = jnp.broadcast_to(lane, (8, LANES))
        for t in range(0, size, 8):
            value = pick_lanes(rims[t : t + 8], lane)
            for g in range(groups):
                value = jnp.where(block == g, pick_lanes(got[g, t : t + 8, :], lane), value)
            picked[k, t : t + 8, :] = value


def stiff_into(out_ref, stiffness, picked):
    entries, size, _, _ = stiffness.shape

    def eight(step, carry):
        first = pl.multiple_of(step * 8, 8)
        accs = [jnp.zeros((16, LANES), F32) for _ in range(8)]
        for k in range(entries):
            for t in range(0, size, 16):
                value = picked[k, t : t + 16, :]
                for r in range(8):
                    accs[r] += stiffness[k, first + r, t : t + 16, :].astype(F32) * value
        out_ref[pl.ds(first, 8), :] = tile_sum(accs)
        return carry

    lax.fori_loop(0, size // 8, eight, 0)


def stiff_body(counts, got, columns, stiffness, basis, inverse, *refs, others, pairs, width):
    vectors = refs[:others]
    image, solved, table, picked, sums = refs[others:]
    pick_columns(got, columns, vectors[0], picked, width)
    stiff_into(image, stiffness, picked)
    project_into(sums, basis, image[...])
    block_product(solved, inverse, image[...])
    named = list(vectors) + [image, solved]
    dots = [total(named[a][...], named[b][...]) for a, b in pairs]
    write_table(table, sums, counts[0], basis.shape[0], dots)


def closing_body(counts, table, coarse, scalars, mine, weights, out_table, out_scalars):
    modes = coarse.shape[0]
    totals = coarse_weights(weights, table, coarse, counts[2])
    e1, z1y1, z1q0, z0y1, r1s, y1s, q0s, r1m0, y1m0, q0m0 = (
        spread(totals, modes + i) for i in range(10)
    )
    e0, z0q0, step0 = scalars[0:1, :], scalars[1:2, :], scalars[2:3, :]
    beta = e1 / e0
    step = e1 / (z1y1 + beta * (z1q0 + z0y1) + beta * beta * z0q0)
    p_y1 = own_row(table, counts[1])
    p_q1 = p_y1 + beta * mine[1:2, :]
    side = jnp.broadcast_to(step * p_q1 - mine[0:1, :], (8, LANES))
    share = jnp.dot(
        side[:, :modes], weights[...], precision=precise, preferred_element_type=F32
    )
    out_table[...] = jnp.broadcast_to(share[0:1, :], out_table.shape)
    q1m1 = y1s + beta * (y1m0 + q0s) + beta * beta * q0m0
    known = step * q1m1 - (z1y1 + beta * z1q0) - (r1s + beta * r1m0)
    rows = [e1, beta, step, step0, known, jnp.zeros((3, LANES), F32)]
    out_scalars[...] = jnp.concatenate(rows, axis=0)


def finish_body(
    scalars,
    weights,
    basis,
    search0,
    image0,
    answer0,
    residual1,
    search1,
    image1,
    solved1,
    solution_out,
    residual_out,
    search_out,
    direction,
):
    beta, step, step0 = scalars[1:2, :], scalars[2:3, :], scalars[3:4, :]
    direction[...] = search1[...] + beta * search0[...]
    solution_out[...] = step0 * search0[...] + step * direction[...]
    residual_out[...] = residual1[...] - step * (image1[...] + beta * image0[...])
    answer1 = solved1[...] + expand(weights, basis)
    search_out[...] = search1[...] - step * (answer1 + beta * answer0[...])


def last_body(table, scalars, search, direction, out):
    e1, step, known = scalars[0:1, :], scalars[2:3, :], scalars[4:5, :]
    shares = jnp.sum(table[...], axis=0, keepdims=True)
    energy = e1 + step * (shares + known)
    out[...] = search[...] + energy / e1 * direction[...]


def local(
    right_side,
    stiffness,
    columns,
    margin_rows,
    local_inverse,
    margin_inverse,
    basis,
    coarse_counts,
    coarse_inverse,
):
    slabs, groups = lax.axis_size("slab"), lax.axis_size("grp")
    width = margin_rows.shape[2]
    size, rows = right_side.shape
    modes = basis.shape[0]
    half = groups // 2
    depth = size * width // LANES
    slab = lax.axis_index("slab")
    place = jnp.stack([lax.axis_index("grp"), slab]).astype(I32)
    counts = jnp.stack([coarse_counts[0], slab, coarse_counts[0]]).astype(I32)

    def pairs(low_step):
        found = []
        for s in range(slabs):
            for g in range(groups):
                other = s + (low_step if g < half else -low_step)
                if 0 <= other < slabs:
                    found.append((s * groups + g, other * groups + g))
        return found

    def exchange(table, axes):
        peers = table.shape[0]
        return lax.all_to_all(table.reshape(peers, 1, LANES), axes, 0, 0).reshape(peers, LANES)

    def gather(rim, send):
        rim = lax.ppermute(rim, AXES, pairs(-1))
        send = send.at[:, size:, :].set(jnp.broadcast_to(rim, (groups, depth, LANES)))
        return lax.all_to_all(send, "grp", 0, 0)

    field, table_of = ((size, rows), F32), ((slabs * groups, LANES), F32)
    small, rim_of = ((8, LANES), F32), ((depth, LANES), F32)
    send_of = ((groups, size + depth, LANES), F32)
    sums = pltpu.VMEM((LANES, LANES), F32)
    weights_of = pltpu.VMEM((modes, LANES), F32)
    picked = pltpu.VMEM((columns.shape[0], size, LANES), F32)

    table, packed, meta = call(
        begin_body,
        [table_of, ((size, depth, LANES), F32), ((8, LANES), I32)],
        [SMEM] * 3 + [VMEM] * 3,
        place,
        margin_rows,
        counts,
        right_side,
        basis,
        margin_inverse,
        scratch=[sums],
        groups=groups,
        rows=rows,
    )
    table = exchange(table, AXES)
    packed = lax.ppermute(packed, AXES, pairs(1))
    inverse, solved = call(
        inverse_body,
        [((size, size, rows), F32), field],
        [VMEM] * 4,
        meta,
        local_inverse,
        packed,
        right_side,
        width=width,
    )
    z0, mine, rim, send = call(
        first_body,
        [field, small, rim_of, send_of],
        [SMEM] * 2 + [VMEM] * 5,
        place,
        counts,
        table,
        coarse_inverse,
        basis,
        solved,
        meta,
        scratch=[weights_of],
        width=width,
    )

    def stiff(got, vectors, dots):
        return call(
            stiff_body,
            [field, field, table_of],
            [SMEM] + [VMEM] * (5 + len(vectors)),
            counts,
            got,
            columns,
            stiffness,
            basis,
            inverse,
            *vectors,
            scratch=[picked, sums],
            others=len(vectors),
            pairs=dots,
            width=width,
        )

    q0, solved, table = stiff(gather(rim, send), [z0, right_side], [(1, 0), (0, 2)])
    m0, r1, z1, mine, scalars, rim, send = call(
        second_body,
        [field, field, field, small, small, rim_of, send_of],
        [SMEM] * 2 + [VMEM] * 9,
        place,
        counts,
        exchange(table, AXES),
        coarse_inverse,
        basis,
        solved,
        meta,
        right_side,
        z0,
        q0,
        mine,
        scratch=[weights_of],
        width=width,
    )
    dots = [(1, 0), (0, 5), (0, 3), (2, 5), (1, 6), (5, 6), (3, 6), (1, 4), (5, 4), (3, 4)]
    y1, solved, table = stiff(gather(rim, send), [z1, r1, z0, q0, m0], dots)
    weights, table, scalars = call(
        closing_body,
        [((modes, LANES), F32), ((slabs, LANES), F32), small],
        [SMEM] + [VMEM] * 4,
        counts,
        exchange(table, AXES),
        coarse_inverse,
        scalars,
        mine,
    )
    x2, r2, z2, d1 = call(
        finish_body,
        [field] * 4,
        [VMEM] * 10,
        scalars,
        weights,
        basis,
        z0,
        q0,
        m0,
        r1,
        z1,
        y1,
        solved,
    )
    (d2,) = call(
        last_body, [field], [VMEM] * 4, exchange(table, "slab"), scalars, z2, d1
    )
    return x2, r2, d2


def solution(mesh):
    in_specs = (
        P(None, AXES),
        P(None, None, None, AXES),
        P(None, AXES),
        P("slab", None, None),
        P(None, None, AXES),
        P(None, None, "slab"),
        P(None, None, AXES),
        P("slab"),
        P("slab", None),
    )
    out_specs = (P(None, AXES),) * 3
    return jax.shard_map(local, mesh=mesh, in_specs=in_specs, out_specs=out_specs, check_vma=False)
```

```python
import functools

import jax
import jax.numpy as jnp
from jax import lax
from jax.experimental import pallas as pl
from jax.experimental.pallas import tpu as pltpu
from jax.sharding import Mesh, PartitionSpec as P

SLAB = ("plane", "core")
AXES = SLAB + ("grp",)
F32, I32 = jnp.float32, jnp.int32
LANES = 128
MIB = 1 << 20
FLOPS = 4 * 10**9
VMEM = pl.BlockSpec(memory_space=pltpu.VMEM)
SMEM = pl.BlockSpec(memory_space=pltpu.SMEM)
HBM = pl.BlockSpec(memory_space=pltpu.HBM)
precise = lax.Precision.HIGHEST


def call(body, outs, specs, *operands, scratch=(), vmem=16, **static):
    shapes = [jax.ShapeDtypeStruct(shape, dtype) for shape, dtype in outs]
    read = sum(x.size * x.dtype.itemsize for x in operands)
    return pl.pallas_call(
        functools.partial(body, **static),
        out_shape=shapes,
        in_specs=specs,
        out_specs=[VMEM] * len(shapes),
        scratch_shapes=list(scratch),
        compiler_params=pltpu.CompilerParams(vmem_limit_bytes=vmem * MIB),
        cost_estimate=pl.CostEstimate(flops=FLOPS, bytes_accessed=read, transcendentals=0),
    )(*operands)


def tile_sum(parts):
    row = lax.broadcasted_iota(I32, (8, LANES), 0)
    sums = []
    for low, high in zip(parts[:4], parts[4:]):
        kept, moved = jnp.where(row < 4, low, high), jnp.where(row < 4, high, low)
        sums.append(kept + pltpu.roll(moved, 4, 0))
    for shift in (2, 1):
        half = len(sums) // 2
        sums = [
            jnp.where(
                row & shift == 0,
                low + pltpu.roll(low, 8 - shift, 0),
                high + pltpu.roll(high, shift, 0),
            )
            for low, high in zip(sums[:half], sums[half:])
        ]
    return sums[0]


def lane_index(rows=8):
    return lax.broadcasted_iota(I32, (rows, LANES), 1)


def pick_lanes(block, index):
    index = jnp.broadcast_to(index, block.shape)
    return jnp.take_along_axis(block, index, axis=1, mode="promise_in_bounds")


def total(a, b):
    return jnp.sum(a * b, axis=0, keepdims=True)


def project_into(sums_ref, basis_ref, vector):
    modes, size, _ = basis_ref.shape

    def eight(step, carry):
        first = pl.multiple_of(step * 8, 8)
        parts = []
        for r in range(8):
            acc = jnp.zeros((16, LANES), F32)
            for t in range(0, size, 16):
                acc += basis_ref[first + r, t : t + 16, :].astype(F32) * vector[t : t + 16]
            parts.append(acc[:8] + acc[8:])
        sums_ref[pl.ds(first, 8), :] = tile_sum(parts)
        return carry

    lax.fori_loop(0, modes // 8, eight, 0)


def block_product(out_ref, blocks_ref, vector):
    size = blocks_ref.shape[0]

    def eight(step, carry):
        first = pl.multiple_of(step * 8, 8)
        parts = []
        for r in range(8):
            acc = jnp.zeros((8, LANES), F32)
            for t in range(0, size, 8):
                acc += blocks_ref[first + r, t : t + 8, :] * vector[t : t + 8]
            parts.append(acc)
        out_ref[pl.ds(first, 8), :] = tile_sum(parts)
        return carry

    lax.fori_loop(0, size // 8, eight, 0)


def write_table(table_ref, sums_ref, count, modes, dots):
    rest = LANES - modes
    rows = dots + [jnp.zeros((1, LANES), F32)] * (rest - len(dots))
    sums_ref[modes:, :] = jnp.concatenate(rows, axis=0)
    row = lax.dot_general(
        jnp.ones((8, LANES), F32),
        sums_ref[...],
        (((1,), (1,)), ((), ())),
        precision=precise,
        preferred_element_type=F32,
    )
    lane = lane_index()
    row = jnp.where((lane < count) | (lane >= modes), row, 0.0)
    for m in range(table_ref.shape[0] // 8):
        table_ref[8 * m : 8 * m + 8, :] = row


def begin_body(
    margin_rows,
    counts,
    field_hbm,
    basis_hbm,
    margin_hbm,
    table,
    packed,
    meta,
    sums,
    field,
    basis,
    margin,
    sems,
    *,
    groups,
    rows,
):
    pairs = [(field_hbm, field), (basis_hbm, basis), (margin_hbm, margin)]
    copies = [pltpu.make_async_copy(a, b, sems.at[i]) for i, (a, b) in enumerate(pairs)]
    for copy in copies:
        copy.start()
    size = field.shape[0]
    width = margin_rows.shape[2]
    group = lax.axis_index("grp")
    face = jnp.where(group < groups // 2, 0, 1)
    lane = lane_index(1)
    slot, owned = jnp.zeros((1, LANES), I32), jnp.zeros((1, LANES), I32)
    source = jnp.full((1, LANES), -1, I32)
    for t in range(width):
        row = margin_rows[0, face, t] - group * rows
        hit = lane == row
        slot = jnp.where(hit, t, slot)
        owned = jnp.where(hit, 1, owned)
        source = jnp.where(lane % width == t, row, source)
    inside = ((source >= 0) & (source < rows)).astype(I32)
    source = jnp.clip(source, 0, rows - 1)
    meta[...] = jnp.concatenate([slot, owned, source, inside, jnp.zeros((4, LANES), I32)], axis=0)

    copies[0].wait()
    copies[1].wait()
    project_into(sums, basis, field[...])
    write_table(table, sums, counts[0], basis.shape[0], [])
    copies[2].wait()
    parts = LANES // width
    depth = size // parts
    given = lax.broadcasted_iota(I32, (margin.shape[2], LANES), 0)
    lanes = lane_index(margin.shape[2])
    place = given == lanes % width + jnp.where(face == 0, width, 0)
    result = jnp.zeros((size * depth, LANES), F32)
    for a in range(parts):
        block = margin[:, a * depth : (a + 1) * depth, :].reshape(size * depth, margin.shape[2])
        chosen = (place & (lanes // width == a)).astype(F32).astype(jnp.bfloat16)
        result += jnp.dot(block, chosen, preferred_element_type=F32)
    packed[...] = result.reshape(size, depth, LANES)


def inverse_body(meta, local_inverse, packed, field, inverse, solved, *, width):
    size, depth, _ = packed.shape
    row = lax.broadcasted_iota(I32, (LANES, LANES), 0)
    place = (row % width == meta[0:1, :]) & (meta[1:2, :] > 0)
    blocks = packed[...].reshape(size * depth, LANES).astype(jnp.bfloat16)
    for a in range(size // depth):
        chosen = (place & (row // width == a)).astype(F32).astype(jnp.bfloat16)
        extra = jnp.dot(blocks, chosen, preferred_element_type=F32)
        own = local_inverse[:, a * depth : (a + 1) * depth, :].astype(F32)
        inverse[:, a * depth : (a + 1) * depth, :] = own + extra.reshape(size, depth, LANES)
    block_product(solved, inverse, field[...])


def coarse_weights(weights_ref, mine, other, coarse, count):
    modes = coarse.shape[0]
    lane = lane_index()
    accs = [jnp.zeros((8, LANES), F32) for _ in range(modes // 8)]
    totals = jnp.zeros((8, LANES), F32)
    first = lax.axis_index("core") == 0
    for m in range(mine.shape[0] // 8):
        own, twin = mine[8 * m : 8 * m + 8, :], other[8 * m : 8 * m + 8, :]
        totals += own + twin
        even, odd = jnp.where(first, own, twin), jnp.where(first, twin, own)
        both = jnp.where(lane < modes, even, pltpu.roll(odd, modes, 1))
        both = jnp.sum(both, axis=0, keepdims=True)
        for r in range(modes // 8):
            accs[r] += coarse[8 * r : 8 * r + 8, LANES * m : LANES * m + LANES] * both
    weights = jnp.dot(
        jnp.concatenate(accs, axis=0),
        jnp.ones((LANES, LANES), F32),
        precision=precise,
        preferred_element_type=F32,
    )
    rows = lax.broadcasted_iota(I32, (modes, LANES), 0)
    weights_ref[...] = jnp.where(rows < count, weights, 0.0)
    return jnp.sum(totals, axis=0, keepdims=True)


def expand(weights_ref, basis):
    modes, size, _ = basis.shape

    def eight(step, accs):
        first = pl.multiple_of(step * 8, 8)
        weights = weights_ref[pl.ds(first, 8), :]
        accs = list(accs)
        for r in range(8):
            weight = weights[r : r + 1, :]
            for t in range(size // 16):
                accs[t] += basis[first + r, 16 * t : 16 * t + 16, :].astype(F32) * weight
        return tuple(accs)

    accs = tuple(jnp.zeros((16, LANES), F32) for _ in range(size // 16))
    return jnp.concatenate(lax.fori_loop(0, modes // 8, eight, accs), axis=0)


def own_row(table):
    start = pl.multiple_of(lax.axis_index("plane") * 8, 8)
    return jnp.sum(table[pl.ds(start, 8), :], axis=0, keepdims=True)


def spread(row, lane):
    return jnp.broadcast_to(row[:, lane : lane + 1], (1, LANES))


def send_out(vector, meta, rim, send, *, width):
    size = vector.shape[0]
    depth = rim.shape[0]
    picked = pick_lanes(vector, meta[2:3, :])
    picked = jnp.where(jnp.broadcast_to(meta[3:4, :], picked.shape) > 0, picked, 0.0)
    lanes = lane_index(depth)
    result = jnp.zeros((depth, LANES), F32)
    for a in range(size // depth):
        part = picked[a * depth : (a + 1) * depth]
        result = jnp.where((lanes >= a * width) & (lanes < (a + 1) * width), part, result)
    rim[...] = result
    for g in range(send.shape[0]):
        send[g, :size, :] = vector
        send[g, size:, :] = result


def first_body(
    counts, table, other, coarse, basis, solved, meta, search, mine, rim, send, weights, *, width
):
    coarse_weights(weights, table, other, coarse, counts[0])
    mine[...] = jnp.broadcast_to(own_row(table), (8, LANES))
    search[...] = solved[...] + expand(weights, basis)
    send_out(search[...], meta, rim, send, width=width)


def second_body(
    counts,
    table,
    other,
    coarse,
    basis,
    solved,
    meta,
    field,
    search,
    image,
    mine0,
    answer,
    residual,
    search1,
    mine,
    scalars,
    rim,
    send,
    weights,
    *,
    width,
):
    modes = basis.shape[0]
    totals = coarse_weights(weights, table, other, coarse, counts[0])
    energy, curve = spread(totals, modes), spread(totals, modes + 1)
    step = energy / curve
    p_q0 = own_row(table)
    p_r1 = mine0[0:1, :] - step * p_q0
    mine[...] = jnp.concatenate([p_r1, p_q0, jnp.zeros((6, LANES), F32)], axis=0)
    scalars[...] = jnp.concatenate([energy, curve, step, jnp.zeros((5, LANES), F32)], axis=0)
    answer[...] = solved[...] + expand(weights, basis)
    residual[...] = field[...] - step * image[...]
    search1[...] = search[...] - step * answer[...]
    send_out(search1[...], meta, rim, send, width=width)


def pick_columns(got, columns, own, picked, width):
    groups, _, _ = got.shape
    size = own.shape[0]
    rows = LANES
    depth = got.shape[1] - size
    half = groups // 2
    upper = sum(got[g, size:, :] for g in range(half))
    lower = sum(got[g, size:, :] for g in range(half, groups))
    lanes = lane_index(depth)
    rims = []
    for a in range(size // depth):
        low = pltpu.roll(lower, (-a * width) % LANES, 1)
        high = pltpu.roll(upper, (width - a * width) % LANES, 1)
        rims.append(jnp.where(lanes < width, low, high))
    rims = jnp.concatenate(rims, axis=0)
    picked[0] = own[...]
    for k in range(1, columns.shape[0]):
        named = columns[k : k + 1, :] - width
        block = named // rows
        lane = named - block * rows
        inside = (named >= 0) & (named < groups * rows)
        rim_lane = jnp.where(named < 0, named + width, named - groups * rows + width)
        lane = jnp.where(inside, lane, rim_lane)
        block = jnp.broadcast_to(jnp.where(inside, block, groups), (8, LANES))
        lane = jnp.broadcast_to(lane, (8, LANES))
        for t in range(0, size, 8):
            value = pick_lanes(rims[t : t + 8], lane)
            for g in range(groups):
                value = jnp.where(block == g, pick_lanes(got[g, t : t + 8, :], lane), value)
            picked[k, t : t + 8, :] = value


def stiff_into(out_ref, stiffness, picked):
    entries, size, _, _ = stiffness.shape

    def eight(step, carry):
        first = pl.multiple_of(step * 8, 8)
        accs = [jnp.zeros((16, LANES), F32) for _ in range(8)]
        for k in range(entries):
            for t in range(0, size, 16):
                value = picked[k, t : t + 16, :]
                for r in range(8):
                    accs[r] += stiffness[k, first + r, t : t + 16, :].astype(F32) * value
        out_ref[pl.ds(first, 8), :] = tile_sum([acc[:8] + acc[8:] for acc in accs])
        return carry

    lax.fori_loop(0, size // 8, eight, 0)


def stiff_body(counts, got, columns, stiffness, basis, inverse, *refs, others, pairs, width):
    vectors = refs[:others]
    image, solved, table, picked, sums = refs[others:]
    pick_columns(got, columns, vectors[0], picked, width)
    stiff_into(image, stiffness, picked)
    project_into(sums, basis, image[...])
    block_product(solved, inverse, image[...])
    named = list(vectors) + [image, solved]
    dots = [total(named[a][...], named[b][...]) for a, b in pairs]
    write_table(table, sums, counts[0], basis.shape[0], dots)


def closing_body(counts, table, other, coarse, scalars, mine, weights, out_table, out_scalars):
    modes = coarse.shape[0]
    totals = coarse_weights(weights, table, other, coarse, counts[0])
    e1, z1y1, z1q0, z0y1, r1s, y1s, q0s, r1m0, y1m0, q0m0 = (
        spread(totals, modes + i) for i in range(10)
    )
    e0, z0q0, step0 = scalars[0:1, :], scalars[1:2, :], scalars[2:3, :]
    beta = e1 / e0
    step = e1 / (z1y1 + beta * (z1q0 + z0y1) + beta * beta * z0q0)
    p_y1 = own_row(table)
    p_q1 = p_y1 + beta * mine[1:2, :]
    side = jnp.broadcast_to(step * p_q1 - mine[0:1, :], (8, LANES))
    share = jnp.dot(
        side[:, :modes], weights[...], precision=precise, preferred_element_type=F32
    )
    out_table[...] = jnp.broadcast_to(share[0:1, :], out_table.shape)
    q1m1 = y1s + beta * (y1m0 + q0s) + beta * beta * q0m0
    known = step * q1m1 - (z1y1 + beta * z1q0) - (r1s + beta * r1m0)
    rows = [e1, beta, step, step0, known, jnp.zeros((3, LANES), F32)]
    out_scalars[...] = jnp.concatenate(rows, axis=0)


def finish_body(
    scalars,
    weights,
    basis,
    search0,
    image0,
    answer0,
    residual1,
    search1,
    image1,
    solved1,
    solution_out,
    residual_out,
    search_out,
    direction,
):
    beta, step, step0 = scalars[1:2, :], scalars[2:3, :], scalars[3:4, :]
    direction[...] = search1[...] + beta * search0[...]
    solution_out[...] = step0 * search0[...] + step * direction[...]
    residual_out[...] = residual1[...] - step * (image1[...] + beta * image0[...])
    answer1 = solved1[...] + expand(weights, basis)
    search_out[...] = search1[...] - step * (answer1 + beta * answer0[...])


def last_body(table, scalars, search, direction, out):
    e1, step, known = scalars[0:1, :], scalars[2:3, :], scalars[4:5, :]
    shares = jnp.sum(table[...], axis=0, keepdims=True)
    energy = e1 + step * (shares + known)
    out[...] = search[...] + energy / e1 * direction[...]


def local(
    right_side,
    stiffness,
    columns,
    margin_rows,
    local_inverse,
    margin_inverse,
    basis,
    coarse_counts,
    coarse_inverse,
):
    planes, groups = lax.axis_size("plane"), lax.axis_size("grp")
    slabs = planes * lax.axis_size("core")
    width = margin_rows.shape[2]
    size, rows = right_side.shape
    modes = basis.shape[0]
    half = groups // 2
    depth = size * width // LANES
    counts = coarse_counts

    def pairs(low_step):
        found = []
        for s in range(slabs):
            for g in range(groups):
                other = s + (low_step if g < half else -low_step)
                if 0 <= other < slabs:
                    found.append((s * groups + g, other * groups + g))
        return found

    def exchange(table, axes):
        peers = table.shape[0]
        return lax.all_to_all(table.reshape(peers, 1, LANES), axes, 0, 0).reshape(peers, LANES)

    def share(table):
        table = exchange(table, ("plane", "grp"))
        return table, lax.ppermute(table, "core", ((0, 1), (1, 0)))

    def gather(rim, send):
        rim = lax.ppermute(rim, AXES, pairs(-1))
        send = send.at[:, size:, :].set(jnp.broadcast_to(rim, (groups, depth, LANES)))
        return lax.all_to_all(send, "grp", 0, 0)

    field, table_of = ((size, rows), F32), ((planes * groups, LANES), F32)
    small, rim_of = ((8, LANES), F32), ((depth, LANES), F32)
    send_of = ((groups, size + depth, LANES), F32)
    sums = pltpu.VMEM((LANES, LANES), F32)
    weights_of = pltpu.VMEM((modes, LANES), F32)
    picked = pltpu.VMEM((columns.shape[0], size, LANES), F32)

    table, packed, meta = call(
        begin_body,
        [table_of, ((size, depth, LANES), F32), ((8, LANES), I32)],
        [SMEM] * 2 + [HBM] * 3,
        margin_rows,
        counts,
        right_side,
        basis,
        margin_inverse,
        scratch=[sums]
        + [pltpu.VMEM(x.shape, x.dtype) for x in (right_side, basis, margin_inverse)]
        + [pltpu.SemaphoreType.DMA((3,))],
        vmem=62,
        groups=groups,
        rows=rows,
    )
    table, other = share(table)
    packed = lax.ppermute(packed, AXES, pairs(1))
    inverse, solved = call(
        inverse_body,
        [((size, size, rows), F32), field],
        [VMEM] * 4,
        meta,
        local_inverse,
        packed,
        right_side,
        width=width,
    )
    z0, mine, rim, send = call(
        first_body,
        [field, small, rim_of, send_of],
        [SMEM] + [VMEM] * 6,
        counts,
        table,
        other,
        coarse_inverse,
        basis,
        solved,
        meta,
        scratch=[weights_of],
        width=width,
    )

    def stiff(got, vectors, dots):
        return call(
            stiff_body,
            [field, field, table_of],
            [SMEM] + [VMEM] * (5 + len(vectors)),
            counts,
            got,
            columns,
            stiffness,
            basis,
            inverse,
            *vectors,
            scratch=[picked, sums],
            others=len(vectors),
            pairs=dots,
            width=width,
        )

    q0, solved, table = stiff(gather(rim, send), [z0, right_side], [(1, 0), (0, 2)])
    m0, r1, z1, mine, scalars, rim, send = call(
        second_body,
        [field, field, field, small, small, rim_of, send_of],
        [SMEM] + [VMEM] * 10,
        counts,
        *share(table),
        coarse_inverse,
        basis,
        solved,
        meta,
        right_side,
        z0,
        q0,
        mine,
        scratch=[weights_of],
        width=width,
    )
    dots = [(1, 0), (0, 5), (0, 3), (2, 5), (1, 6), (5, 6), (3, 6), (1, 4), (5, 4), (3, 4)]
    y1, solved, table = stiff(gather(rim, send), [z1, r1, z0, q0, m0], dots)
    weights, table, scalars = call(
        closing_body,
        [((modes, LANES), F32), ((slabs, LANES), F32), small],
        [SMEM] + [VMEM] * 5,
        counts,
        *share(table),
        coarse_inverse,
        scalars,
        mine,
    )
    x2, r2, z2, d1 = call(
        finish_body,
        [field] * 4,
        [VMEM] * 10,
        scalars,
        weights,
        basis,
        z0,
        q0,
        m0,
        r1,
        z1,
        y1,
        solved,
    )
    (d2,) = call(
        last_body, [field], [VMEM] * 4, exchange(table, SLAB), scalars, z2, d1
    )
    return x2, r2, d2


def solution(mesh):
    slabs, groups = mesh.devices.shape
    mesh = Mesh(mesh.devices.reshape(slabs // 2, 2, groups), AXES)
    in_specs = (
        P(None, AXES),
        P(None, None, None, AXES),
        P(None, AXES),
        P(SLAB, None, None),
        P(None, None, AXES),
        P(None, None, SLAB),
        P(None, None, AXES),
        P(SLAB),
        P(SLAB, None),
    )
    out_specs = (P(None, AXES),) * 3
    return jax.shard_map(local, mesh=mesh, in_specs=in_specs, out_specs=out_specs, check_vma=False)
```

```python
import functools

import jax
import jax.numpy as jnp
from jax import lax
from jax.experimental import pallas as pl
from jax.experimental.pallas import tpu as pltpu
from jax.sharding import Mesh, PartitionSpec as P

SLAB = ("plane", "core")
AXES = SLAB + ("grp",)
F32, I32 = jnp.float32, jnp.int32
LANES = 128
MIB = 1 << 20
FLOPS = 4 * 10**9
VMEM = pl.BlockSpec(memory_space=pltpu.VMEM)
SMEM = pl.BlockSpec(memory_space=pltpu.SMEM)
HBM = pl.BlockSpec(memory_space=pltpu.HBM)
precise = lax.Precision.HIGHEST


def call(body, outs, specs, *operands, scratch=(), vmem=16, **static):
    shapes = [jax.ShapeDtypeStruct(shape, dtype) for shape, dtype in outs]
    read = sum(x.size * x.dtype.itemsize for x in operands)
    return pl.pallas_call(
        functools.partial(body, **static),
        out_shape=shapes,
        in_specs=specs,
        out_specs=[VMEM] * len(shapes),
        scratch_shapes=list(scratch),
        compiler_params=pltpu.CompilerParams(vmem_limit_bytes=vmem * MIB),
        cost_estimate=pl.CostEstimate(flops=FLOPS, bytes_accessed=read, transcendentals=0),
    )(*operands)


def tile_sum(parts):
    row = lax.broadcasted_iota(I32, (8, LANES), 0)
    sums = []
    for low, high in zip(parts[:4], parts[4:]):
        kept, moved = jnp.where(row < 4, low, high), jnp.where(row < 4, high, low)
        sums.append(kept + pltpu.roll(moved, 4, 0))
    for shift in (2, 1):
        half = len(sums) // 2
        sums = [
            jnp.where(
                row & shift == 0,
                low + pltpu.roll(low, 8 - shift, 0),
                high + pltpu.roll(high, shift, 0),
            )
            for low, high in zip(sums[:half], sums[half:])
        ]
    return sums[0]


def lane_index(rows=8):
    return lax.broadcasted_iota(I32, (rows, LANES), 1)


def pick_lanes(block, index):
    index = jnp.broadcast_to(index, block.shape)
    return jnp.take_along_axis(block, index, axis=1, mode="promise_in_bounds")


def total(a, b):
    return jnp.sum(a * b, axis=0, keepdims=True)


def project_into(sums_ref, basis_ref, vector, copy_of=None):
    modes, size, _ = basis_ref.shape

    def eight(step, carry):
        first = pl.multiple_of(step * 8, 8)
        if copy_of:
            copy_of(step).wait()
        parts = []
        for r in range(8):
            acc = jnp.zeros((16, LANES), F32)
            for t in range(0, size, 16):
                acc += basis_ref[first + r, t : t + 16, :].astype(F32) * vector[t : t + 16]
            parts.append(acc[:8] + acc[8:])
        sums_ref[pl.ds(first, 8), :] = tile_sum(parts)
        return carry

    lax.fori_loop(0, modes // 8, eight, 0)


def block_product(out_ref, blocks_ref, vector):
    size = blocks_ref.shape[0]

    def eight(step, carry):
        first = pl.multiple_of(step * 8, 8)
        parts = []
        for r in range(8):
            acc = jnp.zeros((8, LANES), F32)
            for t in range(0, size, 8):
                acc += blocks_ref[first + r, t : t + 8, :] * vector[t : t + 8]
            parts.append(acc)
        out_ref[pl.ds(first, 8), :] = tile_sum(parts)
        return carry

    lax.fori_loop(0, size // 8, eight, 0)


def write_table(table_ref, sums_ref, count, modes, dots):
    rest = LANES - modes
    rows = dots + [jnp.zeros((1, LANES), F32)] * (rest - len(dots))
    sums_ref[modes:, :] = jnp.concatenate(rows, axis=0)
    row = lax.dot_general(
        jnp.ones((8, LANES), F32),
        sums_ref[...],
        (((1,), (1,)), ((), ())),
        precision=precise,
        preferred_element_type=F32,
    )
    lane = lane_index()
    row = jnp.where((lane < count) | (lane >= modes), row, 0.0)
    for m in range(table_ref.shape[0] // 8):
        table_ref[8 * m : 8 * m + 8, :] = row


def own_face(margin_rows, groups):
    face = jnp.where(lax.axis_index("grp") < groups // 2, 0, 1)
    return face, jnp.where(face == 0, margin_rows[0, 0:1, :], margin_rows[0, 1:2, :])


def begin_body(
    counts,
    field_hbm,
    basis_hbm,
    margin_hbm,
    table,
    packed,
    sums,
    field,
    basis,
    margin,
    sems,
    *,
    groups,
    width,
):
    size, modes = field.shape[0], basis.shape[0]

    def copy_of(step):
        part = pl.ds(pl.multiple_of(step * 8, 8), 8)
        return pltpu.make_async_copy(basis_hbm.at[part], basis.at[part], sems.at[step])

    field_copy = pltpu.make_async_copy(field_hbm, field, sems.at[modes // 8])
    margin_copy = pltpu.make_async_copy(margin_hbm, margin, sems.at[modes // 8 + 1])
    field_copy.start()
    for step in range(modes // 8):
        copy_of(step).start()
    margin_copy.start()
    face = jnp.where(lax.axis_index("grp") < groups // 2, 0, 1)
    field_copy.wait()
    project_into(sums, basis, field[...], copy_of)
    write_table(table, sums, counts[0], modes, [])
    margin_copy.wait()
    parts = LANES // width
    depth = size // parts
    given = lax.broadcasted_iota(I32, (margin.shape[2], LANES), 0)
    lanes = lane_index(margin.shape[2])
    place = given == lanes % width + jnp.where(face == 0, width, 0)
    result = jnp.zeros((size * depth, LANES), F32)
    for a in range(parts):
        block = margin[:, a * depth : (a + 1) * depth, :].reshape(size * depth, margin.shape[2])
        chosen = (place & (lanes // width == a)).astype(F32).astype(jnp.bfloat16)
        result += jnp.dot(block, chosen, preferred_element_type=F32)
    packed[...] = result.reshape(size, depth, LANES)


def inverse_body(margin_rows, local_inverse, packed, field, inverse, solved, *, width, groups):
    size, depth, _ = packed.shape
    rows = field.shape[1]
    _, named = own_face(margin_rows, groups)
    square = (width, width)
    diagonal = lax.broadcasted_iota(I32, square, 0) == lax.broadcasted_iota(I32, square, 1)
    owner = jnp.dot(
        jnp.where(diagonal, named.astype(F32), 0.0),
        jnp.ones((width, LANES), F32),
        precision=precise,
        preferred_element_type=F32,
    ).astype(I32)
    owner = jnp.concatenate([owner] * (LANES // width), axis=0)
    row = lax.broadcasted_iota(I32, (LANES, LANES), 0)
    place = owner == lane_index(LANES) + lax.axis_index("grp") * rows
    blocks = packed[...].reshape(size * depth, LANES).astype(jnp.bfloat16)
    for a in range(size // depth):
        chosen = (place & (row // width == a)).astype(F32).astype(jnp.bfloat16)
        extra = jnp.dot(blocks, chosen, preferred_element_type=F32)
        own = local_inverse[:, a * depth : (a + 1) * depth, :].astype(F32)
        inverse[:, a * depth : (a + 1) * depth, :] = own + extra.reshape(size, depth, LANES)
    block_product(solved, inverse, field[...])


def coarse_weights(weights_ref, mine, other, coarse, count):
    modes = coarse.shape[0]
    lane = lane_index()
    accs = [jnp.zeros((8, LANES), F32) for _ in range(modes // 8)]
    totals = jnp.zeros((8, LANES), F32)
    first = lax.axis_index("core") == 0
    for m in range(mine.shape[0] // 8):
        own, twin = mine[8 * m : 8 * m + 8, :], other[8 * m : 8 * m + 8, :]
        totals += own + twin
        even, odd = jnp.where(first, own, twin), jnp.where(first, twin, own)
        both = jnp.where(lane < modes, even, pltpu.roll(odd, modes, 1))
        both = jnp.sum(both, axis=0, keepdims=True)
        for r in range(modes // 8):
            accs[r] += coarse[8 * r : 8 * r + 8, LANES * m : LANES * m + LANES] * both
    weights = jnp.dot(
        jnp.concatenate(accs, axis=0),
        jnp.ones((LANES, LANES), F32),
        precision=precise,
        preferred_element_type=F32,
    )
    rows = lax.broadcasted_iota(I32, (modes, LANES), 0)
    weights_ref[...] = jnp.where(rows < count, weights, 0.0)
    return jnp.sum(totals, axis=0, keepdims=True)


def expand(weights_ref, basis):
    modes, size, _ = basis.shape

    def eight(step, accs):
        first = pl.multiple_of(step * 8, 8)
        weights = weights_ref[pl.ds(first, 8), :]
        accs = list(accs)
        for r in range(8):
            weight = weights[r : r + 1, :]
            for t in range(size // 16):
                accs[t] += basis[first + r, 16 * t : 16 * t + 16, :].astype(F32) * weight
        return tuple(accs)

    accs = tuple(jnp.zeros((16, LANES), F32) for _ in range(size // 16))
    return jnp.concatenate(lax.fori_loop(0, modes // 8, eight, accs), axis=0)


def own_row(table):
    start = pl.multiple_of(lax.axis_index("plane") * 8, 8)
    return jnp.sum(table[pl.ds(start, 8), :], axis=0, keepdims=True)


def spread(row, lane):
    return jnp.broadcast_to(row[:, lane : lane + 1], (1, LANES))


def send_out(vector, margin_rows, rim, send, *, width):
    size, rows = vector.shape
    depth = rim.shape[0]
    _, named = own_face(margin_rows, send.shape[0])
    named = jnp.concatenate([named] * (LANES // width), axis=1) - lax.axis_index("grp") * rows
    inside = ((named >= 0) & (named < rows)).astype(I32)
    picked = pick_lanes(vector, jnp.clip(named, 0, rows - 1))
    picked = jnp.where(jnp.broadcast_to(inside, picked.shape) > 0, picked, 0.0)
    lanes = lane_index(depth)
    result = jnp.zeros((depth, LANES), F32)
    for a in range(size // depth):
        part = picked[a * depth : (a + 1) * depth]
        result = jnp.where((lanes >= a * width) & (lanes < (a + 1) * width), part, result)
    rim[...] = result
    for g in range(send.shape[0]):
        send[g, :size, :] = vector
        send[g, size:, :] = result


def first_body(
    counts,
    table,
    other,
    coarse,
    basis,
    solved,
    margin_rows,
    search,
    mine,
    rim,
    send,
    weights,
    *,
    width,
):
    coarse_weights(weights, table, other, coarse, counts[0])
    mine[...] = jnp.broadcast_to(own_row(table), (8, LANES))
    search[...] = solved[...] + expand(weights, basis)
    send_out(search[...], margin_rows, rim, send, width=width)


def second_body(
    counts,
    table,
    other,
    coarse,
    basis,
    solved,
    margin_rows,
    field,
    search,
    image,
    mine0,
    answer,
    residual,
    search1,
    mine,
    scalars,
    rim,
    send,
    weights,
    *,
    width,
):
    modes = basis.shape[0]
    totals = coarse_weights(weights, table, other, coarse, counts[0])
    energy, curve = spread(totals, modes), spread(totals, modes + 1)
    step = energy / curve
    p_q0 = own_row(table)
    p_r1 = mine0[0:1, :] - step * p_q0
    mine[...] = jnp.concatenate([p_r1, p_q0, jnp.zeros((6, LANES), F32)], axis=0)
    scalars[...] = jnp.concatenate([energy, curve, step, jnp.zeros((5, LANES), F32)], axis=0)
    answer[...] = solved[...] + expand(weights, basis)
    residual[...] = field[...] - step * image[...]
    search1[...] = search[...] - step * answer[...]
    send_out(search1[...], margin_rows, rim, send, width=width)


def pick_columns(got, columns, own, picked, width):
    groups, _, _ = got.shape
    size = own.shape[0]
    rows = LANES
    depth = got.shape[1] - size
    half = groups // 2
    upper = sum(got[g, size:, :] for g in range(half))
    lower = sum(got[g, size:, :] for g in range(half, groups))
    lanes = lane_index(depth)
    rims = []
    for a in range(size // depth):
        low = pltpu.roll(lower, (-a * width) % LANES, 1)
        high = pltpu.roll(upper, (width - a * width) % LANES, 1)
        rims.append(jnp.where(lanes < width, low, high))
    rims = jnp.concatenate(rims, axis=0)
    picked[0] = own[...]
    for k in range(1, columns.shape[0]):
        named = columns[k : k + 1, :] - width
        block = named // rows
        lane = named - block * rows
        inside = (named >= 0) & (named < groups * rows)
        rim_lane = jnp.where(named < 0, named + width, named - groups * rows + width)
        lane = jnp.where(inside, lane, rim_lane)
        block = jnp.broadcast_to(jnp.where(inside, block, groups), (8, LANES))
        lane = jnp.broadcast_to(lane, (8, LANES))
        for t in range(0, size, 8):
            value = pick_lanes(rims[t : t + 8], lane)
            for g in range(groups):
                value = jnp.where(block == g, pick_lanes(got[g, t : t + 8, :], lane), value)
            picked[k, t : t + 8, :] = value


def stiff_into(out_ref, stiffness, picked):
    entries, size, _, _ = stiffness.shape

    def eight(step, carry):
        first = pl.multiple_of(step * 8, 8)
        accs = [jnp.zeros((16, LANES), F32) for _ in range(8)]
        for k in range(entries):
            for t in range(0, size, 16):
                value = picked[k, t : t + 16, :]
                for r in range(8):
                    accs[r] += stiffness[k, first + r, t : t + 16, :].astype(F32) * value
        out_ref[pl.ds(first, 8), :] = tile_sum([acc[:8] + acc[8:] for acc in accs])
        return carry

    lax.fori_loop(0, size // 8, eight, 0)


def stiff_body(counts, got, columns, stiffness, basis, inverse, *refs, others, pairs, width):
    vectors = refs[:others]
    image, solved, table, picked, sums = refs[others:]
    pick_columns(got, columns, vectors[0], picked, width)
    stiff_into(image, stiffness, picked)
    project_into(sums, basis, image[...])
    block_product(solved, inverse, image[...])
    named = list(vectors) + [image, solved]
    dots = [total(named[a][...], named[b][...]) for a, b in pairs]
    write_table(table, sums, counts[0], basis.shape[0], dots)


def closing_body(counts, table, other, coarse, scalars, mine, weights, out_table, out_scalars):
    modes = coarse.shape[0]
    totals = coarse_weights(weights, table, other, coarse, counts[0])
    e1, z1y1, z1q0, z0y1, r1s, y1s, q0s, r1m0, y1m0, q0m0 = (
        spread(totals, modes + i) for i in range(10)
    )
    e0, z0q0, step0 = scalars[0:1, :], scalars[1:2, :], scalars[2:3, :]
    beta = e1 / e0
    step = e1 / (z1y1 + beta * (z1q0 + z0y1) + beta * beta * z0q0)
    p_y1 = own_row(table)
    p_q1 = p_y1 + beta * mine[1:2, :]
    side = jnp.broadcast_to(step * p_q1 - mine[0:1, :], (8, LANES))
    share = jnp.dot(
        side[:, :modes], weights[...], precision=precise, preferred_element_type=F32
    )
    out_table[...] = jnp.broadcast_to(share[0:1, :], out_table.shape)
    q1m1 = y1s + beta * (y1m0 + q0s) + beta * beta * q0m0
    known = step * q1m1 - (z1y1 + beta * z1q0) - (r1s + beta * r1m0)
    rows = [e1, beta, step, step0, known, jnp.zeros((3, LANES), F32)]
    out_scalars[...] = jnp.concatenate(rows, axis=0)


def finish_body(
    scalars,
    weights,
    basis,
    search0,
    image0,
    answer0,
    residual1,
    search1,
    image1,
    solved1,
    solution_out,
    residual_out,
    search_out,
    direction,
):
    beta, step, step0 = scalars[1:2, :], scalars[2:3, :], scalars[3:4, :]
    direction[...] = search1[...] + beta * search0[...]
    solution_out[...] = step0 * search0[...] + step * direction[...]
    residual_out[...] = residual1[...] - step * (image1[...] + beta * image0[...])
    answer1 = solved1[...] + expand(weights, basis)
    search_out[...] = search1[...] - step * (answer1 + beta * answer0[...])


def last_body(table, scalars, search, direction, out):
    e1, step, known = scalars[0:1, :], scalars[2:3, :], scalars[4:5, :]
    shares = jnp.sum(table[...], axis=0, keepdims=True)
    energy = e1 + step * (shares + known)
    out[...] = search[...] + energy / e1 * direction[...]


def local(
    right_side,
    stiffness,
    columns,
    margin_rows,
    local_inverse,
    margin_inverse,
    basis,
    coarse_counts,
    coarse_inverse,
):
    planes, groups = lax.axis_size("plane"), lax.axis_size("grp")
    slabs = planes * lax.axis_size("core")
    width = margin_rows.shape[2]
    size, rows = right_side.shape
    modes = basis.shape[0]
    half = groups // 2
    depth = size * width // LANES
    counts = coarse_counts

    def pairs(low_step):
        found = []
        for s in range(slabs):
            for g in range(groups):
                other = s + (low_step if g < half else -low_step)
                if 0 <= other < slabs:
                    found.append((s * groups + g, other * groups + g))
        return found

    def exchange(table, axes):
        peers = table.shape[0]
        return lax.all_to_all(table.reshape(peers, 1, LANES), axes, 0, 0).reshape(peers, LANES)

    def share(table):
        table = exchange(table, ("plane", "grp"))
        return table, lax.ppermute(table, "core", ((0, 1), (1, 0)))

    def gather(rim, send):
        rim = lax.ppermute(rim, AXES, pairs(-1))
        send = send.at[:, size:, :].set(jnp.broadcast_to(rim, (groups, depth, LANES)))
        return lax.all_to_all(send, "grp", 0, 0)

    field, table_of = ((size, rows), F32), ((planes * groups, LANES), F32)
    small, rim_of = ((8, LANES), F32), ((depth, LANES), F32)
    send_of = ((groups, size + depth, LANES), F32)
    sums = pltpu.VMEM((LANES, LANES), F32)
    weights_of = pltpu.VMEM((modes, LANES), F32)
    picked = pltpu.VMEM((columns.shape[0], size, LANES), F32)

    table, packed = call(
        begin_body,
        [table_of, ((size, depth, LANES), F32)],
        [SMEM] + [HBM] * 3,
        counts,
        right_side,
        basis,
        margin_inverse,
        scratch=[sums]
        + [pltpu.VMEM(x.shape, x.dtype) for x in (right_side, basis, margin_inverse)]
        + [pltpu.SemaphoreType.DMA((modes // 8 + 2,))],
        vmem=62,
        groups=groups,
        width=width,
    )
    table, other = share(table)
    packed = lax.ppermute(packed, AXES, pairs(1))
    inverse, solved = call(
        inverse_body,
        [((size, size, rows), F32), field],
        [VMEM] * 4,
        margin_rows,
        local_inverse,
        packed,
        right_side,
        width=width,
        groups=groups,
    )
    z0, mine, rim, send = call(
        first_body,
        [field, small, rim_of, send_of],
        [SMEM] + [VMEM] * 6,
        counts,
        table,
        other,
        coarse_inverse,
        basis,
        solved,
        margin_rows,
        scratch=[weights_of],
        width=width,
    )

    def stiff(got, vectors, dots):
        return call(
            stiff_body,
            [field, field, table_of],
            [SMEM] + [VMEM] * (5 + len(vectors)),
            counts,
            got,
            columns,
            stiffness,
            basis,
            inverse,
            *vectors,
            scratch=[picked, sums],
            others=len(vectors),
            pairs=dots,
            width=width,
        )

    q0, solved, table = stiff(gather(rim, send), [z0, right_side], [(1, 0), (0, 2)])
    m0, r1, z1, mine, scalars, rim, send = call(
        second_body,
        [field, field, field, small, small, rim_of, send_of],
        [SMEM] + [VMEM] * 10,
        counts,
        *share(table),
        coarse_inverse,
        basis,
        solved,
        margin_rows,
        right_side,
        z0,
        q0,
        mine,
        scratch=[weights_of],
        width=width,
    )
    dots = [(1, 0), (0, 5), (0, 3), (2, 5), (1, 6), (5, 6), (3, 6), (1, 4), (5, 4), (3, 4)]
    y1, solved, table = stiff(gather(rim, send), [z1, r1, z0, q0, m0], dots)
    weights, table, scalars = call(
        closing_body,
        [((modes, LANES), F32), ((slabs, LANES), F32), small],
        [SMEM] + [VMEM] * 5,
        counts,
        *share(table),
        coarse_inverse,
        scalars,
        mine,
    )
    x2, r2, z2, d1 = call(
        finish_body,
        [field] * 4,
        [VMEM] * 10,
        scalars,
        weights,
        basis,
        z0,
        q0,
        m0,
        r1,
        z1,
        y1,
        solved,
    )
    (d2,) = call(
        last_body, [field], [VMEM] * 4, exchange(table, SLAB), scalars, z2, d1
    )
    return x2, r2, d2


def solution(mesh):
    slabs, groups = mesh.devices.shape
    mesh = Mesh(mesh.devices.reshape(slabs // 2, 2, groups), AXES)
    in_specs = (
        P(None, AXES),
        P(None, None, None, AXES),
        P(None, AXES),
        P(SLAB, None, None),
        P(None, None, AXES),
        P(None, None, SLAB),
        P(None, None, AXES),
        P(SLAB),
        P(SLAB, None),
    )
    out_specs = (P(None, AXES),) * 3
    return jax.shard_map(local, mesh=mesh, in_specs=in_specs, out_specs=out_specs, check_vma=False)
```

```python
import functools

import jax
import jax.numpy as jnp
from jax import lax
from jax.experimental import pallas as pl
from jax.experimental.pallas import tpu as pltpu
from jax.sharding import Mesh, PartitionSpec as P

SLAB = ("plane", "core")
AXES = SLAB + ("grp",)
F32, I32 = jnp.float32, jnp.int32
LANES = 128
MIB = 1 << 20
FLOPS = 4 * 10**9
VMEM = pl.BlockSpec(memory_space=pltpu.VMEM)
SMEM = pl.BlockSpec(memory_space=pltpu.SMEM)
HBM = pl.BlockSpec(memory_space=pltpu.HBM)
precise = lax.Precision.HIGHEST


def call(body, outs, specs, *operands, scratch=(), vmem=16, **static):
    shapes = [jax.ShapeDtypeStruct(shape, dtype) for shape, dtype in outs]
    read = sum(x.size * x.dtype.itemsize for x in operands)
    return pl.pallas_call(
        functools.partial(body, **static),
        out_shape=shapes,
        in_specs=specs,
        out_specs=[VMEM] * len(shapes),
        scratch_shapes=list(scratch),
        compiler_params=pltpu.CompilerParams(vmem_limit_bytes=vmem * MIB),
        cost_estimate=pl.CostEstimate(flops=FLOPS, bytes_accessed=read, transcendentals=0),
    )(*operands)


def tile_sum(parts):
    row = lax.broadcasted_iota(I32, (8, LANES), 0)
    sums = []
    for low, high in zip(parts[:4], parts[4:]):
        kept, moved = jnp.where(row < 4, low, high), jnp.where(row < 4, high, low)
        sums.append(kept + pltpu.roll(moved, 4, 0))
    for shift in (2, 1):
        half = len(sums) // 2
        sums = [
            jnp.where(
                row & shift == 0,
                low + pltpu.roll(low, 8 - shift, 0),
                high + pltpu.roll(high, shift, 0),
            )
            for low, high in zip(sums[:half], sums[half:])
        ]
    return sums[0]


def lane_index(rows=8):
    return lax.broadcasted_iota(I32, (rows, LANES), 1)


def pick_lanes(block, index):
    index = jnp.broadcast_to(index, block.shape)
    return jnp.take_along_axis(block, index, axis=1, mode="promise_in_bounds")


def total(a, b):
    return jnp.sum(a * b, axis=0, keepdims=True)


def project_into(sums_ref, basis_ref, vector, copy_of=None):
    modes, size, _ = basis_ref.shape

    def eight(step, carry):
        first = pl.multiple_of(step * 8, 8)
        if copy_of:
            copy_of(step).wait()
        parts = []
        for r in range(8):
            acc = jnp.zeros((16, LANES), F32)
            for t in range(0, size, 16):
                acc += basis_ref[first + r, t : t + 16, :].astype(F32) * vector[t : t + 16]
            parts.append(acc[:8] + acc[8:])
        sums_ref[pl.ds(first, 8), :] = tile_sum(parts)
        return carry

    lax.fori_loop(0, modes // 8, eight, 0)


def block_product(out_ref, blocks_ref, vector):
    size = blocks_ref.shape[0]

    def eight(step, carry):
        first = pl.multiple_of(step * 8, 8)
        parts = []
        for r in range(8):
            acc = jnp.zeros((8, LANES), F32)
            for t in range(0, size, 8):
                acc += blocks_ref[first + r, t : t + 8, :] * vector[t : t + 8]
            parts.append(acc)
        out_ref[pl.ds(first, 8), :] = tile_sum(parts)
        return carry

    lax.fori_loop(0, size // 8, eight, 0)


def write_table(table_ref, sums_ref, count, modes, dots):
    rest = LANES - modes
    rows = dots + [jnp.zeros((1, LANES), F32)] * (rest - len(dots))
    sums_ref[modes:, :] = jnp.concatenate(rows, axis=0)
    lane = lane_index()
    own = lax.broadcasted_iota(I32, (8, LANES), 0)
    acc = jnp.zeros((8, LANES), F32)
    for m in range(0, LANES, 8):
        value = jnp.sum(sums_ref[m : m + 8, :], axis=1, keepdims=True)
        acc += jnp.where(lane == own + m, value, 0.0)
    row = jnp.broadcast_to(jnp.sum(acc, axis=0, keepdims=True), (8, LANES))
    row = jnp.where((lane < count) | (lane >= modes), row, 0.0)
    for m in range(table_ref.shape[0] // 8):
        table_ref[8 * m : 8 * m + 8, :] = row


def own_face(margin_rows, groups):
    face = jnp.where(lax.axis_index("grp") < groups // 2, 0, 1)
    return face, jnp.where(face == 0, margin_rows[0, 0:1, :], margin_rows[0, 1:2, :])


def begin_body(
    counts,
    field_hbm,
    basis_hbm,
    margin_hbm,
    table,
    packed,
    sums,
    field,
    basis,
    margin,
    sems,
    *,
    groups,
    width,
):
    size, modes = field.shape[0], basis.shape[0]

    def copy_of(step):
        part = pl.ds(pl.multiple_of(step * 8, 8), 8)
        return pltpu.make_async_copy(basis_hbm.at[part], basis.at[part], sems.at[step])

    field_copy = pltpu.make_async_copy(field_hbm, field, sems.at[modes // 8])
    margin_copy = pltpu.make_async_copy(margin_hbm, margin, sems.at[modes // 8 + 1])
    field_copy.start()
    for step in range(modes // 8):
        copy_of(step).start()
    margin_copy.start()
    face = jnp.where(lax.axis_index("grp") < groups // 2, 0, 1)
    field_copy.wait()
    project_into(sums, basis, field[...], copy_of)
    write_table(table, sums, counts[0], modes, [])
    margin_copy.wait()
    parts = LANES // width
    depth = size // parts
    given = lax.broadcasted_iota(I32, (margin.shape[2], LANES), 0)
    lanes = lane_index(margin.shape[2])
    place = given == lanes % width + jnp.where(face == 0, width, 0)
    result = jnp.zeros((size * depth, LANES), F32)
    for a in range(parts):
        block = margin[:, a * depth : (a + 1) * depth, :].reshape(size * depth, margin.shape[2])
        chosen = (place & (lanes // width == a)).astype(F32).astype(jnp.bfloat16)
        result += jnp.dot(block, chosen, preferred_element_type=F32)
    packed[...] = result.reshape(size, depth, LANES)


def inverse_body(margin_rows, local_inverse, packed, field, inverse, solved, *, width, groups):
    size, depth, _ = packed.shape
    rows = field.shape[1]
    _, named = own_face(margin_rows, groups)
    square = (width, width)
    diagonal = lax.broadcasted_iota(I32, square, 0) == lax.broadcasted_iota(I32, square, 1)
    owner = jnp.dot(
        jnp.where(diagonal, named.astype(F32), 0.0),
        jnp.ones((width, LANES), F32),
        precision=precise,
        preferred_element_type=F32,
    ).astype(I32)
    owner = jnp.concatenate([owner] * (LANES // width), axis=0)
    row = lax.broadcasted_iota(I32, (LANES, LANES), 0)
    place = owner == lane_index(LANES) + lax.axis_index("grp") * rows
    blocks = packed[...].reshape(size * depth, LANES).astype(jnp.bfloat16)
    for a in range(size // depth):
        chosen = (place & (row // width == a)).astype(F32).astype(jnp.bfloat16)
        extra = jnp.dot(blocks, chosen, preferred_element_type=F32)
        own = local_inverse[:, a * depth : (a + 1) * depth, :].astype(F32)
        inverse[:, a * depth : (a + 1) * depth, :] = own + extra.reshape(size, depth, LANES)
    block_product(solved, inverse, field[...])


def coarse_weights(weights_ref, mine, other, coarse, count):
    modes = coarse.shape[0]
    lane = lane_index(1)
    accs = [jnp.zeros((8, LANES), F32) for _ in range(modes // 8)]
    totals = jnp.zeros((1, LANES), F32)
    first = lax.axis_index("core") == 0
    for m in range(mine.shape[0]):
        own, twin = mine[m : m + 1, :], other[m : m + 1, :]
        totals += own + twin
        even, odd = jnp.where(first, own, twin), jnp.where(first, twin, own)
        both = jnp.where(lane < modes, even, pltpu.roll(odd, modes, 1))
        for r in range(modes // 8):
            accs[r] += coarse[8 * r : 8 * r + 8, LANES * m : LANES * m + LANES] * both
    weights = jnp.sum(jnp.concatenate(accs, axis=0), axis=1, keepdims=True)
    rows = lax.broadcasted_iota(I32, (modes, LANES), 0)
    weights_ref[...] = jnp.where(rows < count, weights, 0.0)
    return totals


def expand(weights_ref, basis):
    modes, size, _ = basis.shape

    def eight(step, accs):
        first = pl.multiple_of(step * 8, 8)
        weights = weights_ref[pl.ds(first, 8), :]
        accs = list(accs)
        for r in range(8):
            weight = weights[r : r + 1, :]
            for t in range(size // 16):
                accs[t] += basis[first + r, 16 * t : 16 * t + 16, :].astype(F32) * weight
        return tuple(accs)

    accs = tuple(jnp.zeros((16, LANES), F32) for _ in range(size // 16))
    return jnp.concatenate(lax.fori_loop(0, modes // 8, eight, accs), axis=0)


def own_row(table):
    return table[pl.ds(lax.axis_index("plane"), 1), :]


def spread(row, lane):
    return jnp.broadcast_to(row[:, lane : lane + 1], (1, LANES))


def send_out(vector, margin_rows, rim, send, *, width):
    size, rows = vector.shape
    depth = rim.shape[0]
    _, named = own_face(margin_rows, send.shape[0])
    named = jnp.concatenate([named] * (LANES // width), axis=1) - lax.axis_index("grp") * rows
    inside = ((named >= 0) & (named < rows)).astype(I32)
    picked = pick_lanes(vector, jnp.clip(named, 0, rows - 1))
    picked = jnp.where(jnp.broadcast_to(inside, picked.shape) > 0, picked, 0.0)
    lanes = lane_index(depth)
    result = jnp.zeros((depth, LANES), F32)
    for a in range(size // depth):
        part = picked[a * depth : (a + 1) * depth]
        result = jnp.where((lanes >= a * width) & (lanes < (a + 1) * width), part, result)
    rim[...] = result
    for g in range(send.shape[0]):
        send[g, :size, :] = vector
        send[g, size:, :] = result


def first_body(
    counts,
    table,
    other,
    coarse,
    basis,
    solved,
    margin_rows,
    search,
    mine,
    rim,
    send,
    weights,
    *,
    width,
):
    coarse_weights(weights, table, other, coarse, counts[0])
    mine[...] = jnp.broadcast_to(own_row(table), (8, LANES))
    search[...] = solved[...] + expand(weights, basis)
    send_out(search[...], margin_rows, rim, send, width=width)


def second_body(
    counts,
    table,
    other,
    coarse,
    basis,
    solved,
    margin_rows,
    field,
    search,
    image,
    mine0,
    answer,
    residual,
    search1,
    mine,
    scalars,
    rim,
    send,
    weights,
    *,
    width,
):
    modes = basis.shape[0]
    totals = coarse_weights(weights, table, other, coarse, counts[0])
    energy, curve = spread(totals, modes), spread(totals, modes + 1)
    step = energy / curve
    p_q0 = own_row(table)
    p_r1 = mine0[0:1, :] - step * p_q0
    mine[...] = jnp.concatenate([p_r1, p_q0, jnp.zeros((6, LANES), F32)], axis=0)
    scalars[...] = jnp.concatenate([energy, curve, step, jnp.zeros((5, LANES), F32)], axis=0)
    answer[...] = solved[...] + expand(weights, basis)
    residual[...] = field[...] - step * image[...]
    search1[...] = search[...] - step * answer[...]
    send_out(search1[...], margin_rows, rim, send, width=width)


def pick_columns(got, columns, own, picked, width):
    groups, _, _ = got.shape
    size = own.shape[0]
    rows = LANES
    depth = got.shape[1] - size
    half = groups // 2
    upper = sum(got[g, size:, :] for g in range(half))
    lower = sum(got[g, size:, :] for g in range(half, groups))
    lanes = lane_index(depth)
    rims = []
    for a in range(size // depth):
        low = pltpu.roll(lower, (-a * width) % LANES, 1)
        high = pltpu.roll(upper, (width - a * width) % LANES, 1)
        rims.append(jnp.where(lanes < width, low, high))
    rims = jnp.concatenate(rims, axis=0)
    picked[0] = own[...]
    for k in range(1, columns.shape[0]):
        named = columns[k : k + 1, :] - width
        block = named // rows
        lane = named - block * rows
        inside = (named >= 0) & (named < groups * rows)
        rim_lane = jnp.where(named < 0, named + width, named - groups * rows + width)
        lane = jnp.where(inside, lane, rim_lane)
        block = jnp.broadcast_to(jnp.where(inside, block, groups), (8, LANES))
        lane = jnp.broadcast_to(lane, (8, LANES))
        for t in range(0, size, 8):
            value = pick_lanes(rims[t : t + 8], lane)
            for g in range(groups):
                value = jnp.where(block == g, pick_lanes(got[g, t : t + 8, :], lane), value)
            picked[k, t : t + 8, :] = value


def stiff_into(out_ref, stiffness, picked):
    entries, size, _, _ = stiffness.shape

    def eight(step, carry):
        first = pl.multiple_of(step * 8, 8)
        accs = [jnp.zeros((16, LANES), F32) for _ in range(8)]
        for k in range(entries):
            for t in range(0, size, 16):
                value = picked[k, t : t + 16, :]
                for r in range(8):
                    accs[r] += stiffness[k, first + r, t : t + 16, :].astype(F32) * value
        out_ref[pl.ds(first, 8), :] = tile_sum([acc[:8] + acc[8:] for acc in accs])
        return carry

    lax.fori_loop(0, size // 8, eight, 0)


def stiff_body(counts, got, columns, stiffness, basis, *refs, others, pairs, width, solve):
    vectors = refs[:others]
    refs = refs[others:]
    if solve:
        inverse, image, table, solved, picked, sums = refs
    else:
        image, table, picked, sums = refs
    pick_columns(got, columns, vectors[0], picked, width)
    stiff_into(image, stiffness, picked)
    project_into(sums, basis, image[...])
    named = list(vectors) + [image]
    if solve:
        block_product(solved, inverse, image[...])
        named.append(solved)
    dots = [total(named[a][...], named[b][...]) for a, b in pairs]
    write_table(table, sums, counts[0], basis.shape[0], dots)


def solve_body(inverse, image, solved):
    block_product(solved, inverse, image[...])


def closing_body(counts, table, other, coarse, scalars, mine, weights, out_table, out_scalars):
    modes = coarse.shape[0]
    totals = coarse_weights(weights, table, other, coarse, counts[0])
    e1, z1y1, z1q0, z0y1, r1s, y1s, q0s, r1m0, y1m0, q0m0 = (
        spread(totals, modes + i) for i in range(10)
    )
    e0, z0q0, step0 = scalars[0:1, :], scalars[1:2, :], scalars[2:3, :]
    beta = e1 / e0
    step = e1 / (z1y1 + beta * (z1q0 + z0y1) + beta * beta * z0q0)
    p_y1 = own_row(table)
    p_q1 = p_y1 + beta * mine[1:2, :]
    side = step * p_q1 - mine[0:1, :]
    place = lax.broadcasted_iota(I32, (modes, LANES), 0) == lane_index(modes)
    share = jnp.sum(jnp.where(place, weights[...] * side, 0.0), axis=0, keepdims=True)
    share = jnp.sum(share, axis=1, keepdims=True)
    out_table[...] = jnp.broadcast_to(share, out_table.shape)
    q1m1 = y1s + beta * (y1m0 + q0s) + beta * beta * q0m0
    known = step * q1m1 - (z1y1 + beta * z1q0) - (r1s + beta * r1m0)
    rows = [e1, beta, step, step0, known, jnp.zeros((3, LANES), F32)]
    out_scalars[...] = jnp.concatenate(rows, axis=0)


def finish_body(
    scalars,
    weights,
    basis,
    search0,
    image0,
    answer0,
    residual1,
    search1,
    image1,
    solved1,
    solution_out,
    residual_out,
    search_out,
    direction,
):
    beta, step, step0 = scalars[1:2, :], scalars[2:3, :], scalars[3:4, :]
    direction[...] = search1[...] + beta * search0[...]
    solution_out[...] = step0 * search0[...] + step * direction[...]
    residual_out[...] = residual1[...] - step * (image1[...] + beta * image0[...])
    answer1 = solved1[...] + expand(weights, basis)
    search_out[...] = search1[...] - step * (answer1 + beta * answer0[...])


def last_body(table, scalars, search, direction, out):
    e1, step, known = scalars[0:1, :], scalars[2:3, :], scalars[4:5, :]
    shares = jnp.sum(table[...], axis=0, keepdims=True)
    energy = e1 + step * (shares + known)
    out[...] = search[...] + energy / e1 * direction[...]


def local(
    right_side,
    stiffness,
    columns,
    margin_rows,
    local_inverse,
    margin_inverse,
    basis,
    coarse_counts,
    coarse_inverse,
):
    planes, groups = lax.axis_size("plane"), lax.axis_size("grp")
    slabs = planes * lax.axis_size("core")
    width = margin_rows.shape[2]
    size, rows = right_side.shape
    modes = basis.shape[0]
    half = groups // 2
    depth = size * width // LANES
    counts = coarse_counts

    def pairs(low_step):
        found = []
        for s in range(slabs):
            for g in range(groups):
                other = s + (low_step if g < half else -low_step)
                if 0 <= other < slabs:
                    found.append((s * groups + g, other * groups + g))
        return found

    def exchange(table, axes):
        peers = table.shape[0]
        return lax.all_to_all(table.reshape(peers, 1, LANES), axes, 0, 0).reshape(peers, LANES)

    def share(table):
        table = exchange(table, ("plane", "grp")).reshape(planes, groups, LANES).sum(axis=1)
        return table, lax.ppermute(table, "core", ((0, 1), (1, 0)))

    def gather(rim, send):
        rim = lax.ppermute(rim, AXES, pairs(-1))
        send = send.at[:, size:, :].set(jnp.broadcast_to(rim, (groups, depth, LANES)))
        return lax.all_to_all(send, "grp", 0, 0)

    field, table_of = ((size, rows), F32), ((planes * groups, LANES), F32)
    small, rim_of = ((8, LANES), F32), ((depth, LANES), F32)
    send_of = ((groups, size + depth, LANES), F32)
    sums = pltpu.VMEM((LANES, LANES), F32)
    weights_of = pltpu.VMEM((modes, LANES), F32)
    picked = pltpu.VMEM((columns.shape[0], size, LANES), F32)

    table, packed = call(
        begin_body,
        [table_of, ((size, depth, LANES), F32)],
        [SMEM] + [HBM] * 3,
        counts,
        right_side,
        basis,
        margin_inverse,
        scratch=[sums]
        + [pltpu.VMEM(x.shape, x.dtype) for x in (right_side, basis, margin_inverse)]
        + [pltpu.SemaphoreType.DMA((modes // 8 + 2,))],
        vmem=62,
        groups=groups,
        width=width,
    )
    table, other = share(table)
    packed = lax.ppermute(packed, AXES, pairs(1))
    inverse, solved = call(
        inverse_body,
        [((size, size, rows), F32), field],
        [VMEM] * 4,
        margin_rows,
        local_inverse,
        packed,
        right_side,
        width=width,
        groups=groups,
    )
    z0, mine, rim, send = call(
        first_body,
        [field, small, rim_of, send_of],
        [SMEM] + [VMEM] * 6,
        counts,
        table,
        other,
        coarse_inverse,
        basis,
        solved,
        margin_rows,
        scratch=[weights_of],
        width=width,
    )

    def stiff(got, vectors, dots, solve):
        return call(
            stiff_body,
            [field, table_of] + [field] * solve,
            [SMEM] + [VMEM] * (4 + len(vectors) + solve),
            counts,
            got,
            columns,
            stiffness,
            basis,
            *vectors,
            *[inverse] * solve,
            scratch=[picked, sums],
            others=len(vectors),
            pairs=dots,
            width=width,
            solve=solve,
        )

    q0, table = stiff(gather(rim, send), [z0, right_side], [(1, 0), (0, 2)], 0)
    (solved,) = call(solve_body, [field], [VMEM] * 2, inverse, q0)
    m0, r1, z1, mine, scalars, rim, send = call(
        second_body,
        [field, field, field, small, small, rim_of, send_of],
        [SMEM] + [VMEM] * 10,
        counts,
        *share(table),
        coarse_inverse,
        basis,
        solved,
        margin_rows,
        right_side,
        z0,
        q0,
        mine,
        scratch=[weights_of],
        width=width,
    )
    dots = [(1, 0), (0, 5), (0, 3), (2, 5), (1, 6), (5, 6), (3, 6), (1, 4), (5, 4), (3, 4)]
    y1, table, solved = stiff(gather(rim, send), [z1, r1, z0, q0, m0], dots, 1)
    weights, table, scalars = call(
        closing_body,
        [((modes, LANES), F32), ((slabs, LANES), F32), small],
        [SMEM] + [VMEM] * 5,
        counts,
        *share(table),
        coarse_inverse,
        scalars,
        mine,
    )
    x2, r2, z2, d1 = call(
        finish_body,
        [field] * 4,
        [VMEM] * 10,
        scalars,
        weights,
        basis,
        z0,
        q0,
        m0,
        r1,
        z1,
        y1,
        solved,
    )
    (d2,) = call(
        last_body, [field], [VMEM] * 4, exchange(table, SLAB), scalars, z2, d1
    )
    return x2, r2, d2


def solution(mesh):
    slabs, groups = mesh.devices.shape
    mesh = Mesh(mesh.devices.reshape(slabs // 2, 2, groups), AXES)
    in_specs = (
        P(None, AXES),
        P(None, None, None, AXES),
        P(None, AXES),
        P(SLAB, None, None),
        P(None, None, AXES),
        P(None, None, SLAB),
        P(None, None, AXES),
        P(SLAB),
        P(SLAB, None),
    )
    out_specs = (P(None, AXES),) * 3
    return jax.shard_map(local, mesh=mesh, in_specs=in_specs, out_specs=out_specs, check_vma=False)
```
